256 devices in a mesh: lat: 64 (over x, z, core), head: 4 (over y).
Axes of the slice: x: 4, y: 4, z: 8, core: 2. Of those that a mesh axis runs over, the one named last changes fastest.
Arguments:
- level_tokens: bfloat16 [32768, 13, 1024], P('lat'), may hold values from -400 to 400
- ln_gain: float32 [1024], replicated, may hold values from 0.25 to 1.75
- key_weight: bfloat16 [1024, 1024], P(None, 'head'), may hold values from -0.1875 to 0.1875
- value_weight: bfloat16 [1024, 1024], P(None, 'head'), may hold values from -0.1875 to 0.1875
- out_weight: bfloat16 [1024, 1024], P('head'), may hold values from -0.1875 to 0.1875
- ocean_queries: bfloat16 [32768, 4, 1024], P('lat', None, 'head'), may hold values from -600 to 600
- send_slots: int32 [64, 64, 8], P('lat'), may hold values from -1 to 511, as said below
Outputs:
- ocean_out: bfloat16 [32768, 4, 1024], P('lat', None, 'head')
The draws below stay inside these ranges and needn't reach their ends.
Inputs may be any that keep to these rules, and one draw needn't show every extreme that they name: `send_slots`: entry [h, o, k] is a patch index within stripe h, or -1 for an empty slot. The live entries of one stripe are distinct, and in each [h, o] row the live entries come first. In every draw some owner has all 8 slots of every stripe live.
All inputs are finite; a program needn't handle non-finite values.
Results may differ from the reference program's by a relative error of at most 0.013.
The reference program's roundings to bfloat16 on the way count: a program that leaves them out, or rounds other values in their place, can miss the bound.
Values may be sent and summed in bfloat16 or wider, within the bound.
A program may use at most 128 MiB of HBM per device.

```python
import math
import jax
import jax.numpy as jnp
from jax import lax

D = 1024
HEAD_DIM = 64
LEV = 13
LATENTS = 4
P_DEV = 512
CAPS = 8
PATCHES = 32768
SLOTS = 32768
N_LAT = 64
N_HEAD = 4


def draw_level_tokens(key, part):
    key = jax.random.fold_in(key, 7)
    key_base, key_cols, key_rows = jax.random.split(key, 3)
    col_scale = jnp.exp(jax.random.uniform(key_cols, (D,), jnp.float32, 0.0, math.log(10.0)))
    row_scale = jnp.exp(jax.random.uniform(key_rows, (PATCHES, LEV, 1), jnp.float32, 0.0, math.log(10.0)))
    base = jnp.clip(jax.random.normal(key_base, (PATCHES, LEV, D), jnp.float32), -4.0, 4.0)
    return (base * col_scale * row_scale).astype(jnp.bfloat16)


def draw_ocean_queries(key, part):
    key = jax.random.fold_in(key, 9)
    key_base = jax.random.fold_in(key, 0)
    base = jnp.clip(jax.random.normal(key_base, (SLOTS, LATENTS, D), jnp.float32), -4.0, 4.0)
    return base.astype(jnp.bfloat16)


def draw_send_slots(key, part):
    key = jax.random.fold_in(key, 11)
    full_owner = jax.random.randint(jax.random.fold_in(key, 1), (), 0, N_LAT)
    stripe = jnp.arange(N_LAT, dtype=jnp.int32)
    distance = jnp.abs(2 * stripe + 1 - N_LAT)
    highest = jnp.maximum(CAPS - (CAPS - CAPS // 4) * distance // N_LAT, 1)
    lowest = highest // 2
    raw_counts = jax.random.randint(jax.random.fold_in(key, 2), (N_LAT, N_LAT), 0, 1 << 20)
    counts = lowest[:, None] + raw_counts % (highest - lowest + 1)[:, None]
    owners = jnp.arange(N_LAT, dtype=jnp.int32)
    counts = jnp.where(owners[None, :] == full_owner, CAPS, counts)
    starts = jnp.cumsum(counts, axis=1) - counts
    stripe_keys = jax.random.split(jax.random.fold_in(key, 3), N_LAT)
    orders = jax.vmap(lambda one_key: jax.random.permutation(one_key, P_DEV))(stripe_keys).astype(jnp.int32)
    within = jnp.arange(CAPS, dtype=jnp.int32)
    position = starts[:, :, None] + within[None, None, :]
    live_slots = within[None, None, :] < counts[:, :, None]
    position = jnp.minimum(position, P_DEV - 1).reshape(N_LAT, N_LAT * CAPS)
    chosen = jnp.take_along_axis(orders, position, axis=1).reshape(N_LAT, N_LAT, CAPS)
    return jnp.where(live_slots, chosen, -1).astype(jnp.int32)


def steps_of(own_key, dims, cuts, smallest, top_value):
    def one(dim, shards_of):
        heights = jax.random.uniform(jax.random.fold_in(jax.random.fold_in(own_key, 6), dim), (shards_of,), jnp.float32, smallest / len(cuts), top_value / len(cuts))
        return jnp.repeat(jnp.exp(heights), dims[dim] // shards_of).reshape((-1,) + (1,) * (len(dims) - dim - 1))

    level = one(*cuts[0])
    for cut in cuts[1:]:
        level = level * one(*cut)
    return level


def normal_values(key, shape, deviation, reach, shards=(), kind=jnp.bfloat16):
    array = deviation * jax.random.normal(key, shape, jnp.float32)
    if shards:
        array = array * steps_of(key, shape, shards, -0.22, 0.18)
    return jnp.clip(array, -reach, reach).astype(kind)


def setup_inputs(seed: int = 0) -> dict:
    seeds = jax.random.split(jax.random.key(seed), 8)
    return {
        "level_tokens": draw_level_tokens(jax.random.fold_in(seeds[7], 71), 0),
        "ln_gain": jnp.clip(1.0 + 0.15 * jax.random.normal(seeds[1], (D,), jnp.float32), 0.25, 1.75),
        "key_weight": normal_values(seeds[2], (D, D), D ** -0.5, 0.1875, ((1, 4),)),
        "value_weight": normal_values(seeds[3], (D, D), D ** -0.5, 0.1875, ((1, 4),)),
        "out_weight": normal_values(seeds[4], (D, D), D ** -0.5, 0.1875, ((0, 4),)),
        "ocean_queries": draw_ocean_queries(jax.random.fold_in(seeds[7], 71), 0),
        "send_slots": draw_send_slots(jax.random.fold_in(seeds[7], 71), 0),
    }


def layer_norm(rows, gain):
    value_matrix = rows.astype(jnp.float32)
    center = lax.optimization_barrier(jnp.mean(value_matrix, axis=-1, keepdims=True))
    max_shifted_scores = value_matrix - center
    spread = lax.optimization_barrier(jnp.mean(max_shifted_scores * max_shifted_scores, axis=-1, keepdims=True))
    return (max_shifted_scores * lax.rsqrt(spread + 1e-05) * gain).astype(jnp.bfloat16)

def reference(level_tokens, ln_gain, key_weight, value_weight, out_weight, ocean_queries, send_slots):
    head_count = D // HEAD_DIM
    group_width = D // N_HEAD
    stripe_base = (jnp.arange(N_LAT, dtype=jnp.int32) * P_DEV)[:, None]

    def owner_block(owner):
        slot_rows = send_slots[:, owner, :]
        live_slots = (slot_rows >= 0).reshape(-1)
        picked = (stripe_base + jnp.maximum(slot_rows, 0)).reshape(-1).astype(jnp.int32)
        gathered = jnp.take(level_tokens, picked, axis=0)
        normalized_rows = layer_norm(gathered, ln_gain).reshape(P_DEV * LEV, D)
        key_rows = jnp.dot(normalized_rows, key_weight, preferred_element_type=jnp.float32).astype(jnp.bfloat16)
        key_rows = key_rows.reshape(P_DEV, LEV, head_count, HEAD_DIM)
        value_rows = jnp.dot(normalized_rows, value_weight, preferred_element_type=jnp.float32).astype(jnp.bfloat16)
        value_rows = value_rows.reshape(P_DEV, LEV, head_count, HEAD_DIM)
        queries = lax.dynamic_slice_in_dim(ocean_queries, (owner * P_DEV).astype(jnp.int32), P_DEV, 0)
        queries = queries.reshape(P_DEV, LATENTS, head_count, HEAD_DIM)
        scores = jnp.einsum('sqhe,slhe->shql', queries.astype(jnp.float32), key_rows.astype(jnp.float32)) / math.sqrt(HEAD_DIM)
        highest = lax.optimization_barrier(jnp.max(scores, axis=-1, keepdims=True))
        expo = jnp.exp(scores - highest)
        soft = (expo / lax.optimization_barrier(jnp.sum(expo, axis=-1, keepdims=True))).astype(jnp.bfloat16)
        mixed_heads = jnp.einsum('shql,slhe->sqhe', soft.astype(jnp.float32), value_rows.astype(jnp.float32)).astype(jnp.bfloat16)
        mixed_heads = mixed_heads.reshape(P_DEV * LATENTS, D)
        summed = jnp.zeros((P_DEV * LATENTS, D), jnp.float32)
        for group_index in range(N_HEAD):
            first_row = group_index * group_width
            partial_term = jnp.dot(mixed_heads[:, first_row:first_row + group_width], out_weight[first_row:first_row + group_width], preferred_element_type=jnp.float32).astype(jnp.bfloat16)
            partial_term = lax.optimization_barrier(partial_term)
            summed = summed + partial_term.astype(jnp.float32)
        result = summed.astype(jnp.bfloat16).reshape(P_DEV, LATENTS, D)
        return jnp.where(live_slots[:, None, None], result, jnp.zeros_like(result))
    blocks = lax.map(owner_block, jnp.arange(N_LAT, dtype=jnp.int32))
    return blocks.reshape(SLOTS, LATENTS, D)
```

```python
import math

import jax
import jax.numpy as jnp
from jax import lax
from jax.sharding import PartitionSpec as P

HEAD_DIM = 64


def normalize(rows, gain):
    value_matrix = rows.astype(jnp.float32)
    center = jnp.mean(value_matrix, axis=-1, keepdims=True)
    shifted = value_matrix - center
    spread = jnp.mean(shifted * shifted, axis=-1, keepdims=True)
    return (shifted * lax.rsqrt(spread + 1e-05) * gain).astype(jnp.bfloat16)


def shards(level_tokens, ln_gain, key_weight, value_weight, out_weight, ocean_queries, send_slots):
    heads = lax.axis_size("head")
    patches, levels, feature_width = level_tokens.shape
    slot_count, latents, local_width = ocean_queries.shape
    head_count = local_width // HEAD_DIM
    arrived = lax.all_to_all(ocean_queries, "lat", split_axis=0, concat_axis=0, tiled=True)
    full_out_weight = lax.all_gather(out_weight, "head", axis=0, tiled=True)
    chosen = send_slots.reshape(-1)
    pick = (chosen[:, None] == jnp.arange(patches, dtype=jnp.int32)[None, :]).astype(jnp.bfloat16)
    normed = normalize(level_tokens, ln_gain)
    key_rows = jnp.einsum("pld,de->ple", normed, key_weight, preferred_element_type=jnp.float32).astype(jnp.bfloat16)
    value_rows = jnp.einsum("pld,de->ple", normed, value_weight, preferred_element_type=jnp.float32).astype(jnp.bfloat16)
    key_rows = key_rows.reshape(patches, levels, head_count, HEAD_DIM)
    value_rows = value_rows.reshape(patches, levels, head_count, HEAD_DIM)
    queries = jnp.einsum("sp,sc->pc", pick, arrived.reshape(slot_count, -1), preferred_element_type=jnp.float32).astype(jnp.bfloat16)
    queries = queries.reshape(patches, latents, head_count, HEAD_DIM)
    scores = jnp.einsum("sqhe,slhe->shql", queries, key_rows, preferred_element_type=jnp.float32) / math.sqrt(HEAD_DIM)
    highest = jnp.max(scores, axis=-1, keepdims=True)
    expo = jnp.exp(scores - highest)
    soft = (expo / jnp.sum(expo, axis=-1, keepdims=True)).astype(jnp.bfloat16)
    mixed = jnp.einsum("shql,slhe->sqhe", soft, value_rows, preferred_element_type=jnp.float32).astype(jnp.bfloat16)
    mixed = jnp.einsum("sp,pc->sc", pick, mixed.reshape(patches, latents * local_width), preferred_element_type=jnp.float32).astype(jnp.bfloat16)
    rows = slot_count // heads
    mixed = mixed.reshape(heads, rows * latents, local_width)
    mixed = lax.all_to_all(mixed, "head", split_axis=0, concat_axis=0, tiled=True)
    terms = jnp.einsum("gre,ged->grd", mixed, full_out_weight.reshape(heads, local_width, feature_width), preferred_element_type=jnp.float32).astype(jnp.bfloat16)
    terms = lax.optimization_barrier(terms)
    summed = jnp.sum(terms.astype(jnp.float32), axis=0).astype(jnp.bfloat16)
    summed = summed.reshape(rows * latents, heads, local_width).swapaxes(0, 1)
    summed = lax.all_to_all(summed, "head", split_axis=0, concat_axis=0, tiled=True)
    summed = summed.reshape(slot_count, latents, local_width)
    return lax.all_to_all(summed, "lat", split_axis=0, concat_axis=0, tiled=True)


def solution(mesh):
    return jax.shard_map(
        shards,
        mesh=mesh,
        in_specs=(
            P("lat", None, None),
            P(),
            P(None, "head"),
            P(None, "head"),
            P("head", None),
            P("lat", None, "head"),
            P("lat", None, None),
        ),
        out_specs=P("lat", None, "head"),
        check_vma=False,
    )
```

```python
import functools
import math

import jax
import jax.numpy as jnp
from jax import lax
from jax.experimental import pallas as pl
from jax.experimental.pallas import tpu as pltpu
from jax.sharding import PartitionSpec as P

HEAD_DIM = 64
CORES = 2
ROWS = 32
MESH = pl.DeviceIdType.MESH


def attend_kernel(
    dims,
    index_ref,
    token_ref,
    gain_ref,
    key_weight_ref,
    value_weight_ref,
    out_weight_ref,
    query_ref,
    out_ref,
    token_buf,
    normed,
    pick,
    keys,
    values,
    query_buf,
    mix_send,
    mix_recv,
    weight_buf,
    out_stage,
    token_sem,
    query_send_sem,
    query_recv_sem,
    mix_send_sem,
    mix_recv_sem,
    weight_send_sem,
    weight_recv_sem,
    out_send_sem,
    out_recv_sem,
):
    nx, nz, ny, caps, latents = dims
    levels, patches, width = token_ref.shape
    local_width = key_weight_ref.shape[1]
    head_count = local_width // HEAD_DIM
    peers = nx * nz * CORES
    high = nz // ny
    block = caps * latents
    share = high * CORES * block
    chunk = nz * CORES * block
    me, my_head = lax.axis_index("lat"), lax.axis_index("head")
    my_x = lax.div(me, nz * CORES)
    my_z = lax.rem(lax.div(me, CORES), nz)
    my_core = lax.rem(me, CORES)

    def offset(dx, place):
        head = lax.div(place, high * CORES)
        upper = lax.rem(lax.div(place, CORES), high)
        return lax.rem(head + dx, ny) + ny * upper, lax.rem(place, CORES)

    def ahead(dx, dz, dc):
        return (lax.rem(my_x + dx, nx) * nz + lax.rem(my_z + dz, nz)) * CORES + lax.rem(my_core + dc, CORES)

    def behind(dx, dz, dc):
        return (lax.rem(my_x - dx + nx, nx) * nz + lax.rem(my_z - dz + nz, nz)) * CORES + lax.rem(
            my_core + dc, CORES
        )

    def token_copy(level, slot):
        return pltpu.make_async_copy(token_ref.at[level], token_buf.at[slot], token_sem.at[slot])

    token_copy(0, 0).start()

    barrier = pltpu.get_barrier_semaphore()

    def greet(head, dx, place):
        dz, dc = offset(dx, place)
        pl.semaphore_signal(barrier, inc=1, device_id=(behind(dx, dz, dc), head), device_id_type=MESH)

    for dx in range(nx):

        @pl.loop(1 if dx == 0 else 0, nz * CORES)
        def _(place, dx=dx):
            dz, dc = offset(dx, place)
            pl.semaphore_signal(barrier, inc=1, device_id=(ahead(dx, dz, dc), my_head), device_id_type=MESH)

    for step in range(1, ny):
        head = lax.rem(my_head + step, ny)
        pl.semaphore_signal(barrier, inc=1, device_id=(me, head), device_id_type=MESH)
        for dx in range(nx):

            @pl.loop(0, high * CORES)
            def _(place, dx=dx, head=head):
                greet(head, dx, head * (high * CORES) + place)

    pl.semaphore_wait(barrier, (peers - 1) + (ny - 1) + (ny - 1) * nx * high * CORES)

    own_queries = pltpu.make_async_copy(
        query_ref.at[pl.ds(pl.multiple_of(me * block, block), block)],
        query_buf.at[0, pl.ds(0, block)],
        query_recv_sem.at[0],
    )
    own_queries.start()
    for dx in range(nx):

        @pl.loop(1 if dx == 0 else 0, nz * CORES)
        def _(place, dx=dx):
            dz, dc = offset(dx, place)
            stripe = behind(dx, dz, dc)
            pltpu.make_async_remote_copy(
                src_ref=query_ref.at[pl.ds(pl.multiple_of(stripe * block, block), block)],
                dst_ref=query_buf.at[dx, pl.ds(pl.multiple_of(place * block, block), block)],
                send_sem=query_send_sem,
                recv_sem=query_recv_sem.at[dx],
                device_id=(stripe, my_head),
                device_id_type=MESH,
            ).start()

    def weight_copy(step):
        return pltpu.make_async_remote_copy(
            src_ref=out_weight_ref,
            dst_ref=weight_buf.at[step - 1],
            send_sem=weight_send_sem.at[step - 1],
            recv_sem=weight_recv_sem.at[step - 1],
            device_id=(me, lax.rem(my_head - step + ny, ny)),
            device_id_type=MESH,
        )

    for step in range(1, ny):
        weight_copy(step).start()

    for dx in range(nx):

        @pl.loop(0, nz)
        def _(pair, dx=dx):
            dz, _ = offset(dx, pair * CORES)
            first, second = ahead(dx, dz, 0), ahead(dx, dz, 1)
            index = jnp.concatenate(
                [
                    index_ref[pl.ds(pl.multiple_of(first * caps, caps), caps), :],
                    index_ref[pl.ds(pl.multiple_of(second * caps, caps), caps), :],
                ],
                axis=0,
            )
            lane = lax.broadcasted_iota(jnp.int32, index.shape, 1)
            row = pl.multiple_of((dx * nz + pair) * (CORES * caps), CORES * caps)
            for tile in range(0, patches, 128):
                hit = (index == lane + tile).astype(jnp.float32)
                pick[pl.ds(row, CORES * caps), tile : tile + 128] = hit[:, : min(128, patches - tile)].astype(
                    jnp.bfloat16
                )

    @pl.loop(0, levels)
    def _(level):
        slot = lax.rem(level, 2)
        token_copy(level, slot).wait()

        @pl.when(level + 1 < levels)
        def _():
            token_copy(level + 1, 1 - slot).start()

        @pl.loop(0, patches // ROWS)
        def _(step):
            rows = pl.ds(pl.multiple_of(step * ROWS, ROWS), ROWS)
            raw = token_buf[slot, rows, :].astype(jnp.float32)
            shifted = raw - jnp.sum(raw, axis=1, keepdims=True) * (1.0 / width)
            spread = jnp.sum(shifted * shifted, axis=1, keepdims=True) * (1.0 / width)
            normed[rows, :] = (shifted * lax.rsqrt(spread + 1e-05) * gain_ref[...]).astype(jnp.bfloat16)

        for weight_ref, kept in ((key_weight_ref, keys), (value_weight_ref, values)):
            projected = jnp.dot(normed[...], weight_ref[...], preferred_element_type=jnp.float32)
            kept[level] = jnp.dot(
                pick[...], projected.astype(jnp.bfloat16), preferred_element_type=jnp.float32
            ).astype(jnp.bfloat16)

    group = CORES * caps
    group_rows = group * latents

    def attend(dx):
        whole = query_buf.at[dx]
        pltpu.make_async_copy(whole, whole, query_recv_sem.at[dx]).wait()

        @pl.loop(0, nz)
        def _(pair):
            slots = pl.ds(pl.multiple_of((dx * nz + pair) * group, group), group)
            rows = pl.ds(pl.multiple_of(pair * group_rows, group_rows), group_rows)
            group_keys = keys[:, slots, :].reshape(levels * group, local_width)
            group_values = values[:, slots, :].reshape(levels * group, local_width)
            queries = query_buf[dx, rows, :]
            lane_head = lax.broadcasted_iota(jnp.int32, (1, local_width), 1) // HEAD_DIM
            by_head = jnp.concatenate(
                [queries * (lane_head == h).astype(jnp.float32).astype(jnp.bfloat16) for h in range(head_count)],
                axis=0,
            )
            scores = lax.dot_general(
                group_keys, by_head, (((1,), (1,)), ((), ())), preferred_element_type=jnp.float32
            ).reshape(levels, group, head_count * group_rows)
            highest = jnp.max(scores, axis=0, keepdims=True)
            expo = jnp.exp2((scores - highest) * (math.log2(math.e) / math.sqrt(HEAD_DIM)))
            total = jnp.sum(expo, axis=0)
            shape = (group, head_count * group_rows)
            column_slot = (lax.broadcasted_iota(jnp.int32, shape, 1) % group_rows) // latents
            own = lax.broadcasted_iota(jnp.int32, shape, 0) == column_slot
            share_of = jnp.where(own, 1.0 / total, 0.0)
            soft = (expo * share_of[None]).astype(jnp.bfloat16).reshape(levels * group, head_count * group_rows)
            mixed = lax.dot_general(
                soft, group_values, (((0,), (0,)), ((), ())), preferred_element_type=jnp.float32
            )
            result = mixed[:group_rows]
            for h in range(1, head_count):
                result = jnp.where(lane_head == h, mixed[h * group_rows : (h + 1) * group_rows], result)
            mix_send[dx, rows, :] = result.astype(jnp.bfloat16)

        for step in range(1, ny):
            head = lax.rem(my_head - step + ny, ny)
            pltpu.make_async_remote_copy(
                src_ref=mix_send.at[dx, pl.ds(pl.multiple_of(head * share, share), share)],
                dst_ref=mix_recv.at[dx, step - 1],
                send_sem=mix_send_sem,
                recv_sem=mix_recv_sem.at[dx],
                device_id=(me, head),
                device_id_type=MESH,
            ).start()

    def out_copy(dx, place, head):
        dz, dc = offset(dx, my_head * (high * CORES) + place)
        return pltpu.make_async_remote_copy(
            src_ref=out_stage.at[dx, head, pl.ds(pl.multiple_of(place * block, block), block)],
            dst_ref=out_ref.at[pl.ds(pl.multiple_of(me * block, block), block)],
            send_sem=out_send_sem,
            recv_sem=out_recv_sem,
            device_id=(ahead(dx, dz, dc), head),
            device_id_type=MESH,
        )

    def project(dx):
        whole = mix_recv.at[dx]
        pltpu.make_async_copy(whole, whole, mix_recv_sem.at[dx]).wait()
        if dx == 0:
            for step in range(1, ny):
                weight_copy(step).wait_recv()
        own = mix_send[dx, pl.ds(pl.multiple_of(my_head * share, share), share), :]
        for head in range(ny):
            columns = slice(head * local_width, (head + 1) * local_width)
            term = jnp.dot(own, out_weight_ref[:, columns], preferred_element_type=jnp.float32)
            summed = term.astype(jnp.bfloat16).astype(jnp.float32)
            for step in range(1, ny):
                term = jnp.dot(
                    mix_recv[dx, step - 1], weight_buf[step - 1, :, columns], preferred_element_type=jnp.float32
                )
                summed += term.astype(jnp.bfloat16).astype(jnp.float32)
            out_stage[dx, head] = summed.astype(jnp.bfloat16)
        if dx == 0:

            @pl.when(my_head == 0)
            def _():
                pltpu.make_async_copy(
                    out_stage.at[0, 0, pl.ds(0, block)],
                    out_ref.at[pl.ds(pl.multiple_of(me * block, block), block)],
                    out_recv_sem,
                ).start()

            @pl.when(my_head != 0)
            def _():
                out_copy(0, 0, 0).start()

        @pl.loop(1 if dx == 0 else 0, high * CORES * ny)
        def _(step):
            out_copy(dx, lax.div(step, ny), lax.rem(step, ny)).start()

    for dx in range(nx):
        attend(dx)
        if dx >= 1:
            project(dx - 1)
    project(nx - 1)

    def drain(ref, sem):
        pltpu.make_async_copy(ref, ref, sem).wait()

    drain(query_ref.at[pl.ds(0, (peers - 1) * block)], query_send_sem)
    for step in range(1, ny):
        weight_copy(step).wait_send()
    drain(mix_send.at[:, pl.ds(0, (ny - 1) * share)], mix_send_sem)
    drain(out_ref.at[pl.ds(0, (peers - 1) * block)], out_send_sem)

    @pl.when(my_head != 0)
    def _():
        drain(out_ref.at[pl.ds(0, block)], out_send_sem)

    drain(out_ref, out_recv_sem)


def shards(sizes, level_tokens, ln_gain, key_weight, value_weight, out_weight, ocean_queries, send_slots):
    nx, nz, ny = sizes
    patches, levels, width = level_tokens.shape
    slot_count, latents, local_width = ocean_queries.shape
    caps = send_slots.shape[2]
    block = caps * latents
    share = nz // ny * CORES * block
    chunk = nz * CORES * block
    index = jnp.broadcast_to(send_slots.reshape(slot_count, 1), (slot_count, 128))
    vmem = pl.BlockSpec(memory_space=pltpu.VMEM)
    anywhere = pl.BlockSpec(memory_space=pl.ANY)
    bf16 = jnp.bfloat16
    dma = pltpu.SemaphoreType.DMA
    result = pl.pallas_call(
        functools.partial(attend_kernel, (nx, nz, ny, caps, latents)),
        out_shape=jax.ShapeDtypeStruct((slot_count * latents, local_width), bf16),
        in_specs=[vmem, anywhere, vmem, vmem, vmem, vmem, anywhere],
        out_specs=anywhere,
        scratch_shapes=[
            pltpu.VMEM((2, patches, width), bf16),
            pltpu.VMEM((patches, width), bf16),
            pltpu.VMEM((slot_count, patches), bf16),
            pltpu.VMEM((levels, slot_count, local_width), bf16),
            pltpu.VMEM((levels, slot_count, local_width), bf16),
            pltpu.VMEM((nx, chunk, local_width), bf16),
            pltpu.VMEM((nx, chunk, local_width), bf16),
            pltpu.VMEM((nx, ny - 1, share, local_width), bf16),
            pltpu.VMEM((ny - 1, local_width, width), bf16),
            pltpu.VMEM((nx, ny, share, local_width), bf16),
            dma((2,)),
            dma,
            dma((nx,)),
            dma,
            dma((nx,)),
            dma((ny - 1,)),
            dma((ny - 1,)),
            dma,
            dma,
        ],
        compiler_params=pltpu.CompilerParams(
            collective_id=0, has_side_effects=True, vmem_limit_bytes=48 * 1024 * 1024
        ),
    )(
        index,
        level_tokens.transpose(1, 0, 2),
        ln_gain.reshape(1, width),
        key_weight,
        value_weight,
        out_weight,
        ocean_queries.reshape(slot_count * latents, local_width),
    )
    return result.reshape(slot_count, latents, local_width)


def solution(mesh):
    ny = mesh.shape["head"]
    nz = 2 * ny
    nx = mesh.shape["lat"] // (nz * CORES)
    return jax.shard_map(
        functools.partial(shards, (nx, nz, ny)),
        mesh=mesh,
        in_specs=(
            P("lat", None, None),
            P(),
            P(None, "head"),
            P(None, "head"),
            P("head", None),
            P("lat", None, "head"),
            P("lat", None, None),
        ),
        out_specs=P("lat", None, "head"),
        check_vma=False,
    )
```

```python
import functools
import math

import jax
import jax.numpy as jnp
from jax import lax
from jax.experimental import pallas as pl
from jax.experimental.pallas import tpu as pltpu
from jax.sharding import PartitionSpec as P

HEAD_DIM = 64
CORES = 2
ROWS = 32
MESH = pl.DeviceIdType.MESH


def attend_kernel(
    dims,
    index_ref,
    token_ref,
    gain_ref,
    key_weight_ref,
    value_weight_ref,
    out_weight_ref,
    query_ref,
    out_ref,
    token_buf,
    projection,
    normed,
    pick,
    projected,
    keys,
    values,
    query_buf,
    mix_send,
    mix_recv,
    weight_buf,
    out_stage,
    token_sem,
    projection_sem,
    query_send_sem,
    query_recv_sem,
    mix_send_sem,
    mix_recv_sem,
    weight_send_sem,
    weight_recv_sem,
    pair_send_sem,
    pair_recv_sem,
    out_send_sem,
    out_recv_sem,
):
    nx, nz, ny, caps, latents = dims
    levels, patches, width = token_ref.shape
    local_width = key_weight_ref.shape[1]
    head_count = local_width // HEAD_DIM
    peers = nx * nz * CORES
    high = nz // ny
    block = caps * latents
    share = high * CORES * block
    chunk = nz * CORES * block
    me, my_head = lax.axis_index("lat"), lax.axis_index("head")
    my_x = lax.div(me, nz * CORES)
    my_z = lax.rem(lax.div(me, CORES), nz)
    my_core = lax.rem(me, CORES)

    def offset(dx, place):
        head = lax.div(place, high * CORES)
        upper = lax.rem(lax.div(place, CORES), high)
        return lax.rem(head + dx, ny) + ny * upper, lax.rem(place, CORES)

    def ahead(dx, dz, dc):
        return (lax.rem(my_x + dx, nx) * nz + lax.rem(my_z + dz, nz)) * CORES + lax.rem(my_core + dc, CORES)

    def behind(dx, dz, dc):
        return (lax.rem(my_x - dx + nx, nx) * nz + lax.rem(my_z - dz + nz, nz)) * CORES + lax.rem(
            my_core + dc, CORES
        )

    def token_copy(level):
        return pltpu.make_async_copy(token_ref.at[level], token_buf.at[level], token_sem.at[level])

    weight_copies = [
        pltpu.make_async_copy(ref, projection.at[:, pl.ds(at * local_width, local_width)], projection_sem.at[at])
        for at, ref in enumerate((key_weight_ref, value_weight_ref))
    ]
    own_weight = pltpu.make_async_copy(out_weight_ref, weight_buf.at[0], weight_recv_sem.at[0])
    for level in range(levels):
        token_copy(level).start()
    for copy in weight_copies:
        copy.start()
    own_weight.start()

    barrier = pltpu.get_barrier_semaphore()

    def greet(head, dx, place):
        dz, dc = offset(dx, place)
        pl.semaphore_signal(barrier, inc=1, device_id=(behind(dx, dz, dc), head), device_id_type=MESH)

    for dx in range(nx):

        @pl.loop(1 if dx == 0 else 0, nz * CORES)
        def _(place, dx=dx):
            dz, dc = offset(dx, place)
            pl.semaphore_signal(barrier, inc=1, device_id=(ahead(dx, dz, dc), my_head), device_id_type=MESH)

    for step in range(1, ny):
        head = lax.rem(my_head + step, ny)
        pl.semaphore_signal(barrier, inc=1, device_id=(me, head), device_id_type=MESH)
        for dx in range(nx):

            @pl.loop(0, high * CORES)
            def _(place, dx=dx, head=head):
                greet(head, dx, head * (high * CORES) + place)

    chosen = index_ref[...].astype(jnp.float32)
    owner_lane = lax.broadcasted_iota(jnp.int32, chosen.shape, 1)
    patch = lax.broadcasted_iota(jnp.int32, (caps, patches), 1).astype(jnp.float32)

    def hits(owner):
        mine = jnp.sum(jnp.where(owner_lane == owner, chosen, 0.0), axis=1, keepdims=True)
        return (mine == patch).astype(jnp.float32)

    for dx in range(nx):

        @pl.loop(0, nz, unroll=nz)
        def _(pair, dx=dx):
            dz, _ = offset(dx, pair * CORES)
            both = jnp.concatenate([hits(ahead(dx, dz, 0)), hits(ahead(dx, dz, 1))], axis=0)
            row = pl.multiple_of((dx * nz + pair) * (CORES * caps), CORES * caps)
            pick[pl.ds(row, CORES * caps), :] = both.astype(jnp.bfloat16)

    pl.semaphore_wait(barrier, (peers - 1) + (ny - 1) + (ny - 1) * nx * high * CORES)

    own_queries = pltpu.make_async_copy(
        query_ref.at[pl.ds(pl.multiple_of(me * block, block), block)],
        query_buf.at[0, pl.ds(0, block)],
        query_recv_sem.at[0],
    )
    own_queries.start()
    for dx in range(nx):

        @pl.loop(1 if dx == 0 else 0, nz * CORES)
        def _(place, dx=dx):
            dz, dc = offset(dx, place)
            stripe = behind(dx, dz, dc)
            pltpu.make_async_remote_copy(
                src_ref=query_ref.at[pl.ds(pl.multiple_of(stripe * block, block), block)],
                dst_ref=query_buf.at[dx, pl.ds(pl.multiple_of(place * block, block), block)],
                send_sem=query_send_sem,
                recv_sem=query_recv_sem.at[dx],
                device_id=(stripe, my_head),
                device_id_type=MESH,
            ).start()

    half = local_width // CORES
    my_half = pl.ds(pl.multiple_of(my_core * half, half), half)

    def weight_copy(step):
        return pltpu.make_async_remote_copy(
            src_ref=out_weight_ref.at[my_half],
            dst_ref=weight_buf.at[step, my_half],
            send_sem=weight_send_sem.at[step],
            recv_sem=weight_recv_sem.at[step],
            device_id=(me, lax.rem(my_head - step + ny, ny)),
            device_id_type=MESH,
        )

    def pair_copy(step):
        return pltpu.make_async_remote_copy(
            src_ref=weight_buf.at[step, my_half],
            dst_ref=weight_buf.at[step, my_half],
            send_sem=pair_send_sem.at[step],
            recv_sem=pair_recv_sem.at[step],
            device_id=(me + 1 - 2 * my_core, my_head),
            device_id_type=MESH,
        )

    for step in range(1, ny):
        weight_copy(step).start()

    for copy in weight_copies:
        copy.wait()

    @pl.loop(0, levels)
    def _(level):
        token_copy(level).wait()

        @pl.loop(0, patches // ROWS, unroll=patches // ROWS)
        def _(step):
            rows = pl.ds(pl.multiple_of(step * ROWS, ROWS), ROWS)
            raw = token_buf[level, rows, :].astype(jnp.float32)
            shifted = raw - jnp.sum(raw, axis=1, keepdims=True) * (1.0 / width)
            spread = jnp.sum(shifted * shifted, axis=1, keepdims=True) * (1.0 / width)
            normed[rows, :] = (shifted * lax.rsqrt(spread + 1e-05) * gain_ref[...]).astype(jnp.bfloat16)

        projected[...] = jnp.dot(normed[...], projection[...], preferred_element_type=jnp.float32).astype(
            jnp.bfloat16
        )
        ordered = jnp.dot(pick[...], projected[...], preferred_element_type=jnp.float32).astype(jnp.bfloat16)
        keys[level] = ordered[:, :local_width]
        values[level] = ordered[:, local_width:]

    own_weight.wait()
    for step in range(1, ny):
        weight_copy(step).wait_recv()
        pair_copy(step).start()

    group = CORES * caps
    group_rows = group * latents

    def attend(dx):
        whole = query_buf.at[dx]
        pltpu.make_async_copy(whole, whole, query_recv_sem.at[dx]).wait()

        @pl.loop(0, nz, unroll=nz)
        def _(pair):
            slots = pl.ds(pl.multiple_of((dx * nz + pair) * group, group), group)
            rows = pl.ds(pl.multiple_of(pair * group_rows, group_rows), group_rows)
            group_keys = keys[:, slots, :].reshape(levels * group, local_width)
            group_values = values[:, slots, :].reshape(levels * group, local_width)
            queries = query_buf[dx, rows, :]
            lane_head = lax.broadcasted_iota(jnp.int32, (1, local_width), 1) // HEAD_DIM
            by_head = jnp.concatenate(
                [queries * (lane_head == h).astype(jnp.float32).astype(jnp.bfloat16) for h in range(head_count)],
                axis=0,
            )
            scores = lax.dot_general(
                group_keys, by_head, (((1,), (1,)), ((), ())), preferred_element_type=jnp.float32
            ).reshape(levels, group, head_count * group_rows)
            highest = jnp.max(scores, axis=0, keepdims=True)
            expo = jnp.exp2((scores - highest) * (math.log2(math.e) / math.sqrt(HEAD_DIM)))
            total = jnp.sum(expo, axis=0)
            shape = (group, head_count * group_rows)
            column_slot = (lax.broadcasted_iota(jnp.int32, shape, 1) % group_rows) // latents
            own = lax.broadcasted_iota(jnp.int32, shape, 0) == column_slot
            share_of = jnp.where(own, 1.0 / total, 0.0)
            soft = (expo * share_of[None]).astype(jnp.bfloat16).reshape(levels * group, head_count * group_rows)
            mixed = lax.dot_general(
                soft, group_values, (((0,), (0,)), ((), ())), preferred_element_type=jnp.float32
            )
            result = mixed[:group_rows]
            for h in range(1, head_count):
                result = jnp.where(lane_head == h, mixed[h * group_rows : (h + 1) * group_rows], result)
            mix_send[dx, rows, :] = result.astype(jnp.bfloat16)

        for step in range(1, ny):
            head = lax.rem(my_head - step + ny, ny)
            pltpu.make_async_remote_copy(
                src_ref=mix_send.at[dx, pl.ds(pl.multiple_of(head * share, share), share)],
                dst_ref=mix_recv.at[dx, step - 1],
                send_sem=mix_send_sem,
                recv_sem=mix_recv_sem.at[dx],
                device_id=(me, head),
                device_id_type=MESH,
            ).start()

    def out_copy(dx, place, head):
        dz, dc = offset(dx, my_head * (high * CORES) + place)
        return pltpu.make_async_remote_copy(
            src_ref=out_stage.at[dx, head, pl.ds(pl.multiple_of(place * block, block), block)],
            dst_ref=out_ref.at[pl.ds(pl.multiple_of(me * block, block), block)],
            send_sem=out_send_sem,
            recv_sem=out_recv_sem,
            device_id=(ahead(dx, dz, dc), head),
            device_id_type=MESH,
        )

    def project(dx):
        whole = mix_recv.at[dx]
        pltpu.make_async_copy(whole, whole, mix_recv_sem.at[dx]).wait()
        if dx == 0:
            for step in range(1, ny):
                pair_copy(step).wait_recv()
        own = mix_send[dx, pl.ds(pl.multiple_of(my_head * share, share), share), :]
        for head in range(ny):
            columns = slice(head * local_width, (head + 1) * local_width)
            term = jnp.dot(own, weight_buf[0, :, columns], preferred_element_type=jnp.float32)
            summed = term.astype(jnp.bfloat16).astype(jnp.float32)
            for step in range(1, ny):
                term = jnp.dot(
                    mix_recv[dx, step - 1], weight_buf[step, :, columns], preferred_element_type=jnp.float32
                )
                summed += term.astype(jnp.bfloat16).astype(jnp.float32)
            out_stage[dx, head] = summed.astype(jnp.bfloat16)
        if dx == 0:

            @pl.when(my_head == 0)
            def _():
                pltpu.make_async_copy(
                    out_stage.at[0, 0, pl.ds(0, block)],
                    out_ref.at[pl.ds(pl.multiple_of(me * block, block), block)],
                    out_recv_sem,
                ).start()

            @pl.when(my_head != 0)
            def _():
                out_copy(0, 0, 0).start()

        @pl.loop(1 if dx == 0 else 0, high * CORES * ny)
        def _(step):
            out_copy(dx, lax.div(step, ny), lax.rem(step, ny)).start()

    for dx in range(nx):
        attend(dx)
        if dx >= 1:
            project(dx - 1)
    project(nx - 1)

    def drain(ref, sem):
        pltpu.make_async_copy(ref, ref, sem).wait()

    drain(query_ref.at[pl.ds(0, (peers - 1) * block)], query_send_sem)
    for step in range(1, ny):
        weight_copy(step).wait_send()
        pair_copy(step).wait_send()
    drain(mix_send.at[:, pl.ds(0, (ny - 1) * share)], mix_send_sem)
    drain(out_ref.at[pl.ds(0, (peers - 1) * block)], out_send_sem)

    @pl.when(my_head != 0)
    def _():
        drain(out_ref.at[pl.ds(0, block)], out_send_sem)

    drain(out_ref, out_recv_sem)


def shards(sizes, level_tokens, ln_gain, key_weight, value_weight, out_weight, ocean_queries, send_slots):
    nx, nz, ny = sizes
    patches, levels, width = level_tokens.shape
    slot_count, latents, local_width = ocean_queries.shape
    caps = send_slots.shape[2]
    block = caps * latents
    share = nz // ny * CORES * block
    chunk = nz * CORES * block
    vmem = pl.BlockSpec(memory_space=pltpu.VMEM)
    anywhere = pl.BlockSpec(memory_space=pl.ANY)
    bf16 = jnp.bfloat16
    dma = pltpu.SemaphoreType.DMA
    result = pl.pallas_call(
        functools.partial(attend_kernel, (nx, nz, ny, caps, latents)),
        out_shape=jax.ShapeDtypeStruct((slot_count * latents, local_width), bf16),
        in_specs=[vmem, anywhere, vmem, anywhere, anywhere, anywhere, anywhere],
        out_specs=anywhere,
        scratch_shapes=[
            pltpu.VMEM((levels, patches, width), bf16),
            pltpu.VMEM((width, 2 * local_width), bf16),
            pltpu.VMEM((patches, width), bf16),
            pltpu.VMEM((slot_count, patches), bf16),
            pltpu.VMEM((patches, 2 * local_width), bf16),
            pltpu.VMEM((levels, slot_count, local_width), bf16),
            pltpu.VMEM((levels, slot_count, local_width), bf16),
            pltpu.VMEM((nx, chunk, local_width), bf16),
            pltpu.VMEM((nx, chunk, local_width), bf16),
            pltpu.VMEM((nx, ny - 1, share, local_width), bf16),
            pltpu.VMEM((ny, local_width, width), bf16),
            pltpu.VMEM((nx, ny, share, local_width), bf16),
            dma((levels,)),
            dma((2,)),
            dma,
            dma((nx,)),
            dma,
            dma((nx,)),
            dma((ny,)),
            dma((ny,)),
            dma((ny,)),
            dma((ny,)),
            dma,
            dma,
        ],
        compiler_params=pltpu.CompilerParams(
            collective_id=0, has_side_effects=True, vmem_limit_bytes=60 * 1024 * 1024
        ),
    )(
        send_slots.reshape(-1, caps).T,
        level_tokens.transpose(1, 0, 2),
        ln_gain.reshape(1, width),
        key_weight,
        value_weight,
        out_weight,
        ocean_queries.reshape(slot_count * latents, local_width),
    )
    return result.reshape(slot_count, latents, local_width)


def solution(mesh):
    ny = mesh.shape["head"]
    nz = 2 * ny
    nx = mesh.shape["lat"] // (nz * CORES)
    return jax.shard_map(
        functools.partial(shards, (nx, nz, ny)),
        mesh=mesh,
        in_specs=(
            P("lat", None, None),
            P(),
            P(None, "head"),
            P(None, "head"),
            P("head", None),
            P("lat", None, "head"),
            P("lat", None, None),
        ),
        out_specs=P("lat", None, "head"),
        check_vma=False,
    )
```

```python
import functools
import math

import jax
import jax.numpy as jnp
from jax import lax
from jax.experimental import pallas as pl
from jax.experimental.pallas import tpu as pltpu
from jax.sharding import PartitionSpec as P

HEAD_DIM = 64
CORES = 2
MESH = pl.DeviceIdType.MESH


def attend_kernel(
    dims,
    index_ref,
    token_ref,
    gain_ref,
    key_weight_ref,
    value_weight_ref,
    out_weight_ref,
    query_ref,
    out_ref,
    token_buf,
    projection,
    normed,
    pick,
    keys,
    values,
    query_buf,
    mix_send,
    mix_recv,
    weight_buf,
    out_stage,
    token_sem,
    projection_sem,
    query_send_sem,
    query_recv_sem,
    mix_send_sem,
    mix_recv_sem,
    weight_send_sem,
    weight_recv_sem,
    pair_send_sem,
    pair_recv_sem,
    out_send_sem,
    out_recv_sem,
):
    nx, nz, ny, caps, latents = dims
    levels, patches, width = token_ref.shape
    local_width = key_weight_ref.shape[1]
    head_count = local_width // HEAD_DIM
    peers = nx * nz * CORES
    high = nz // ny
    block = caps * latents
    share = high * CORES * block
    chunk = nz * CORES * block
    me, my_head = lax.axis_index("lat"), lax.axis_index("head")
    my_x = lax.div(me, nz * CORES)
    my_z = lax.rem(lax.div(me, CORES), nz)
    my_core = lax.rem(me, CORES)

    def offset(dx, place):
        head = lax.div(place, high * CORES)
        upper = lax.rem(lax.div(place, CORES), high)
        return lax.rem(head + dx, ny) + ny * upper, lax.rem(place, CORES)

    def ahead(dx, dz, dc):
        return (lax.rem(my_x + dx, nx) * nz + lax.rem(my_z + dz, nz)) * CORES + lax.rem(my_core + dc, CORES)

    def behind(dx, dz, dc):
        return (lax.rem(my_x - dx + nx, nx) * nz + lax.rem(my_z - dz + nz, nz)) * CORES + lax.rem(
            my_core + dc, CORES
        )

    def token_copy(level):
        return pltpu.make_async_copy(token_ref.at[level], token_buf.at[level], token_sem.at[level])

    weight_copies = [
        pltpu.make_async_copy(ref, projection.at[:, pl.ds(at * local_width, local_width)], projection_sem.at[at])
        for at, ref in enumerate((key_weight_ref, value_weight_ref))
    ]
    own_weight = pltpu.make_async_copy(out_weight_ref, weight_buf.at[0], weight_recv_sem.at[0])
    for level in range(levels):
        token_copy(level).start()
    for copy in weight_copies:
        copy.start()
    own_weight.start()

    barrier = pltpu.get_barrier_semaphore()

    @pl.loop(1, peers)
    def _(place):
        dx = lax.div(place, nz * CORES)
        dz, dc = offset(dx, lax.rem(place, nz * CORES))
        pl.semaphore_signal(barrier, inc=1, device_id=(ahead(dx, dz, dc), my_head), device_id_type=MESH)

    for step in range(1, ny):
        head = lax.rem(my_head + step, ny)
        pl.semaphore_signal(barrier, inc=1, device_id=(me, head), device_id_type=MESH)

        @pl.loop(0, nx * high * CORES)
        def _(place, head=head):
            dx = lax.div(place, high * CORES)
            dz, dc = offset(dx, head * (high * CORES) + lax.rem(place, high * CORES))
            pl.semaphore_signal(barrier, inc=1, device_id=(behind(dx, dz, dc), head), device_id_type=MESH)

    chosen = index_ref[...].astype(jnp.float32)
    owner_lane = lax.broadcasted_iota(jnp.int32, chosen.shape, 1)
    patch = lax.broadcasted_iota(jnp.int32, (caps, patches), 1).astype(jnp.float32)

    def hits(owner):
        mine = jnp.sum(jnp.where(owner_lane == owner, chosen, 0.0), axis=1, keepdims=True)
        return (mine == patch).astype(jnp.float32)

    @pl.loop(0, nx)
    def _(dx):
        @pl.loop(0, nz, unroll=nz)
        def _(pair):
            dz, _ = offset(dx, pair * CORES)
            both = jnp.concatenate([hits(ahead(dx, dz, 0)), hits(ahead(dx, dz, 1))], axis=0)
            row = pl.multiple_of((dx * nz + pair) * (CORES * caps), CORES * caps)
            pick[pl.ds(row, CORES * caps), :] = both.astype(jnp.bfloat16)

    pl.semaphore_wait(barrier, (peers - 1) + (ny - 1) + (ny - 1) * nx * high * CORES)

    half = local_width // CORES
    my_half = pl.ds(pl.multiple_of(my_core * half, half), half)

    def weight_copy(step):
        return pltpu.make_async_remote_copy(
            src_ref=out_weight_ref.at[my_half],
            dst_ref=weight_buf.at[step, my_half],
            send_sem=weight_send_sem.at[step],
            recv_sem=weight_recv_sem.at[step],
            device_id=(me, lax.rem(my_head - step + ny, ny)),
            device_id_type=MESH,
        )

    def pair_copy(step):
        return pltpu.make_async_remote_copy(
            src_ref=weight_buf.at[step, my_half],
            dst_ref=weight_buf.at[step, my_half],
            send_sem=pair_send_sem.at[step],
            recv_sem=pair_recv_sem.at[step],
            device_id=(me + 1 - 2 * my_core, my_head),
            device_id_type=MESH,
        )

    for step in range(1, ny):
        weight_copy(step).start()

    own_queries = pltpu.make_async_copy(
        query_ref.at[pl.ds(pl.multiple_of(me * caps, caps), caps)],
        query_buf.at[0, pl.ds(0, caps)],
        query_recv_sem.at[0],
    )
    own_queries.start()
    @pl.loop(1, peers)
    def _(place):
        dx, at = lax.div(place, nz * CORES), lax.rem(place, nz * CORES)
        dz, dc = offset(dx, at)
        stripe = behind(dx, dz, dc)
        pltpu.make_async_remote_copy(
            src_ref=query_ref.at[pl.ds(pl.multiple_of(stripe * caps, caps), caps)],
            dst_ref=query_buf.at[dx, pl.ds(pl.multiple_of(at * caps, caps), caps)],
            send_sem=query_send_sem,
            recv_sem=query_recv_sem.at[dx],
            device_id=(stripe, my_head),
            device_id_type=MESH,
        ).start()

    for copy in weight_copies:
        copy.wait()
    for level in range(levels):
        token_copy(level).wait()

    chunk_slots = nz * CORES * caps

    def project_tokens(dx):
        slots = pl.ds(pl.multiple_of(dx * chunk_slots, chunk_slots), chunk_slots)
        parity = lax.rem(dx, 2)

        def normalize(level):
            raw = jnp.dot(pick[slots, :], token_buf[level], preferred_element_type=jnp.float32)
            shifted = raw - jnp.sum(raw, axis=1, keepdims=True) * (1.0 / width)
            spread = jnp.sum(shifted * shifted, axis=1, keepdims=True) * (1.0 / width)
            return (shifted * lax.rsqrt(spread + 1e-05) * gain_ref[...]).astype(jnp.bfloat16)

        def keep(level, at):
            both = jnp.dot(normed[at], projection[...], preferred_element_type=jnp.float32).astype(jnp.bfloat16)
            keys[parity, level] = both[:, :local_width]
            values[parity, level] = both[:, local_width:]

        normed[0] = normalize(0)

        @pl.loop(0, levels // 2, unroll=levels // 2)
        def _(pair):
            for at in range(2):
                following = normalize(2 * pair + at + 1)
                keep(2 * pair + at, at)
                normed[1 - at] = following

        keep(levels - 1, 0)

    group = CORES * caps
    group_rows = group * latents

    def attend(dx):
        parity = lax.rem(dx, 2)
        whole = query_buf.at[dx]
        pltpu.make_async_copy(whole, whole, query_recv_sem.at[dx]).wait()

        @pl.loop(0, nz, unroll=nz)
        def _(pair):
            slots = pl.ds(pl.multiple_of(pair * group, group), group)
            rows = pl.ds(pl.multiple_of(pair * group_rows, group_rows), group_rows)
            group_keys = keys[parity, :, slots, :].reshape(levels * group, local_width)
            group_values = values[parity, :, slots, :].reshape(levels * group, local_width)
            queries = query_buf[dx, slots].reshape(group_rows, local_width)
            lane_head = lax.broadcasted_iota(jnp.int32, (1, local_width), 1) // HEAD_DIM
            by_head = jnp.concatenate(
                [queries * (lane_head == h).astype(jnp.float32).astype(jnp.bfloat16) for h in range(head_count)],
                axis=0,
            )
            scores = lax.dot_general(
                group_keys, by_head, (((1,), (1,)), ((), ())), preferred_element_type=jnp.float32
            ).reshape(levels, group, head_count * group_rows)
            highest = jnp.max(scores, axis=0, keepdims=True)
            expo = jnp.exp2((scores - highest) * (math.log2(math.e) / math.sqrt(HEAD_DIM)))
            total = jnp.sum(expo, axis=0)
            shape = (group, head_count * group_rows)
            column_slot = (lax.broadcasted_iota(jnp.int32, shape, 1) % group_rows) // latents
            own = lax.broadcasted_iota(jnp.int32, shape, 0) == column_slot
            share_of = jnp.where(own, 1.0 / total, 0.0)
            soft = (expo * share_of[None]).astype(jnp.bfloat16).reshape(levels * group, head_count * group_rows)
            mixed = lax.dot_general(
                soft, group_values, (((0,), (0,)), ((), ())), preferred_element_type=jnp.float32
            )
            result = mixed[:group_rows]
            for h in range(1, head_count):
                result = jnp.where(lane_head == h, mixed[h * group_rows : (h + 1) * group_rows], result)
            mix_send[dx, rows, :] = result.astype(jnp.bfloat16)

        for step in range(1, ny):
            head = lax.rem(my_head - step + ny, ny)
            pltpu.make_async_remote_copy(
                src_ref=mix_send.at[dx, pl.ds(pl.multiple_of(head * share, share), share)],
                dst_ref=mix_recv.at[dx, step - 1],
                send_sem=mix_send_sem,
                recv_sem=mix_recv_sem.at[dx],
                device_id=(me, head),
                device_id_type=MESH,
            ).start()

    def out_copy(dx, place, head):
        dz, dc = offset(dx, my_head * (high * CORES) + place)
        return pltpu.make_async_remote_copy(
            src_ref=out_stage.at[dx, head, pl.ds(pl.multiple_of(place * caps, caps), caps)],
            dst_ref=out_ref.at[pl.ds(pl.multiple_of(me * caps, caps), caps)],
            send_sem=out_send_sem,
            recv_sem=out_recv_sem,
            device_id=(ahead(dx, dz, dc), head),
            device_id_type=MESH,
        )

    def project(dx):
        whole = mix_recv.at[dx]
        pltpu.make_async_copy(whole, whole, mix_recv_sem.at[dx]).wait()
        own = mix_send[dx, pl.ds(pl.multiple_of(my_head * share, share), share), :]
        for head in range(ny):
            columns = slice(head * local_width, (head + 1) * local_width)
            term = jnp.dot(own, weight_buf[0, :, columns], preferred_element_type=jnp.float32)
            summed = term.astype(jnp.bfloat16).astype(jnp.float32)
            for step in range(1, ny):
                term = jnp.dot(
                    mix_recv[dx, step - 1], weight_buf[step, :, columns], preferred_element_type=jnp.float32
                )
                summed += term.astype(jnp.bfloat16).astype(jnp.float32)
            out_stage[dx, head] = summed.astype(jnp.bfloat16).reshape(share // latents, latents, local_width)
        own_place = (dx == 0) & (my_head == 0)

        @pl.when(own_place)
        def _():
            pltpu.make_async_copy(
                out_stage.at[0, 0, pl.ds(0, caps)],
                out_ref.at[pl.ds(pl.multiple_of(me * caps, caps), caps)],
                out_recv_sem,
            ).start()

        @pl.when(jnp.logical_not(own_place))
        def _():
            out_copy(dx, 0, 0).start()

        @pl.loop(1, high * CORES * ny)
        def _(step):
            out_copy(dx, lax.div(step, ny), lax.rem(step, ny)).start()

    @pl.loop(0, nx + 1)
    def _(step):
        @pl.when(step < nx)
        def _():
            project_tokens(step)

        @pl.when(step >= 1)
        def _():
            attend(step - 1)

        @pl.when(step == 1)
        def _():
            own_weight.wait()
            for other in range(1, ny):
                weight_copy(other).wait_recv()
                pair_copy(other).start()

        @pl.when(step == 2)
        def _():
            for other in range(1, ny):
                pair_copy(other).wait_recv()

        @pl.when(step >= 2)
        def _():
            project(step - 2)

    if nx == 1:
        for other in range(1, ny):
            pair_copy(other).wait_recv()
    project(nx - 1)

    def drain(ref, sem):
        pltpu.make_async_copy(ref, ref, sem).wait()

    drain(query_ref.at[pl.ds(0, (peers - 1) * caps)], query_send_sem)
    for step in range(1, ny):
        weight_copy(step).wait_send()
        pair_copy(step).wait_send()
    drain(mix_send.at[:, pl.ds(0, (ny - 1) * share)], mix_send_sem)
    drain(out_ref.at[pl.ds(0, (peers - 1) * caps)], out_send_sem)

    @pl.when(my_head != 0)
    def _():
        drain(out_ref.at[pl.ds(0, caps)], out_send_sem)

    drain(out_ref, out_recv_sem)


def shards(sizes, level_tokens, ln_gain, key_weight, value_weight, out_weight, ocean_queries, send_slots):
    nx, nz, ny = sizes
    patches, levels, width = level_tokens.shape
    slot_count, latents, local_width = ocean_queries.shape
    caps = send_slots.shape[2]
    block = caps * latents
    share = nz // ny * CORES * block
    chunk = nz * CORES * block
    vmem = pl.BlockSpec(memory_space=pltpu.VMEM)
    anywhere = pl.BlockSpec(memory_space=pl.ANY)
    stay = pl.BlockSpec(memory_space=pltpu.HBM)
    bf16 = jnp.bfloat16
    dma = pltpu.SemaphoreType.DMA
    return pl.pallas_call(
        functools.partial(attend_kernel, (nx, nz, ny, caps, latents)),
        out_shape=jax.ShapeDtypeStruct((slot_count, latents, local_width), bf16),
        in_specs=[vmem, stay, vmem, stay, stay, stay, anywhere],
        out_specs=anywhere,
        scratch_shapes=[
            pltpu.VMEM((levels, patches, width), bf16),
            pltpu.VMEM((width, 2 * local_width), bf16),
            pltpu.VMEM((2, slot_count // nx, width), bf16),
            pltpu.VMEM((slot_count, patches), bf16),
            pltpu.VMEM((2, levels, slot_count // nx, local_width), bf16),
            pltpu.VMEM((2, levels, slot_count // nx, local_width), bf16),
            pltpu.VMEM((nx, chunk // latents, latents, local_width), bf16),
            pltpu.VMEM((nx, chunk, local_width), bf16),
            pltpu.VMEM((nx, ny - 1, share, local_width), bf16),
            pltpu.VMEM((ny, local_width, width), bf16),
            pltpu.VMEM((nx, ny, share // latents, latents, local_width), bf16),
            dma((levels,)),
            dma((2,)),
            dma,
            dma((nx,)),
            dma,
            dma((nx,)),
            dma((ny,)),
            dma((ny,)),
            dma((ny,)),
            dma((ny,)),
            dma,
            dma,
        ],
        compiler_params=pltpu.CompilerParams(
            collective_id=0, has_side_effects=True, vmem_limit_bytes=60 * 1024 * 1024
        ),
    )(
        send_slots.reshape(-1, caps).T,
        level_tokens.transpose(1, 0, 2),
        ln_gain.reshape(1, width),
        key_weight,
        value_weight,
        out_weight,
        ocean_queries,
    )


def solution(mesh):
    ny = mesh.shape["head"]
    nz = 2 * ny
    nx = mesh.shape["lat"] // (nz * CORES)
    return jax.shard_map(
        functools.partial(shards, (nx, nz, ny)),
        mesh=mesh,
        in_specs=(
            P("lat", None, None),
            P(),
            P(None, "head"),
            P(None, "head"),
            P("head", None),
            P("lat", None, "head"),
            P("lat", None, None),
        ),
        out_specs=P("lat", None, "head"),
        check_vma=False,
    )
```

```python
import functools
import math

import jax
import jax.numpy as jnp
from jax import lax
from jax.experimental import pallas as pl
from jax.experimental.pallas import tpu as pltpu
from jax.sharding import PartitionSpec as P

HEAD_DIM = 64
CORES = 2
MESH = pl.DeviceIdType.MESH


def attend_kernel(
    dims,
    index_ref,
    token_ref,
    gain_ref,
    key_weight_ref,
    value_weight_ref,
    out_weight_ref,
    query_ref,
    out_ref,
    token_buf,
    projection,
    normed,
    pick,
    keys,
    values,
    query_buf,
    mix_send,
    mix_recv,
    weight_buf,
    out_stage,
    token_sem,
    projection_sem,
    query_send_sem,
    query_recv_sem,
    mix_send_sem,
    mix_recv_sem,
    weight_send_sem,
    weight_recv_sem,
    pair_send_sem,
    pair_recv_sem,
    out_send_sem,
    out_recv_sem,
    x_ready,
    heads_ready,
):
    nx, nz, ny, caps, latents = dims
    levels, patches, width = token_ref.shape
    local_width = key_weight_ref.shape[1]
    head_count = local_width // HEAD_DIM
    peers = nx * nz * CORES
    high = nz // ny
    block = caps * latents
    share = high * CORES * block
    chunk = nz * CORES * block
    me, my_head = lax.axis_index("lat"), lax.axis_index("head")
    my_x = lax.div(me, nz * CORES)
    my_z = lax.rem(lax.div(me, CORES), nz)
    my_core = lax.rem(me, CORES)

    def offset(dx, place):
        head = lax.div(place, high * CORES)
        upper = lax.rem(lax.div(place, CORES), high)
        return lax.rem(head + dx, ny) + ny * upper, lax.rem(place, CORES)

    def ahead(dx, dz, dc):
        return (lax.rem(my_x + dx, nx) * nz + lax.rem(my_z + dz, nz)) * CORES + lax.rem(my_core + dc, CORES)

    def behind(dx, dz, dc):
        return (lax.rem(my_x - dx + nx, nx) * nz + lax.rem(my_z - dz + nz, nz)) * CORES + lax.rem(
            my_core + dc, CORES
        )

    def token_copy(level):
        return pltpu.make_async_copy(token_ref.at[level], token_buf.at[level], token_sem.at[level])

    weight_copies = [
        pltpu.make_async_copy(ref, projection.at[:, pl.ds(at * local_width, local_width)], projection_sem.at[at])
        for at, ref in enumerate((key_weight_ref, value_weight_ref))
    ]
    own_weight = pltpu.make_async_copy(out_weight_ref, weight_buf.at[0], weight_recv_sem.at[0])
    for level in range(levels):
        token_copy(level).start()
    for copy in weight_copies:
        copy.start()
    own_weight.start()

    barrier = pltpu.get_barrier_semaphore()

    def meet(semaphore, lat, head):
        pl.semaphore_signal(semaphore, inc=1, device_id=(lat, head), device_id_type=MESH)

    def meet_along_x(semaphore):
        for dx in range(1, nx):
            meet(semaphore, ahead(dx, 0, 0), my_head)

    def meet_heads(semaphore):
        for step in range(1, ny):
            meet(semaphore, me, lax.rem(my_head + step, ny))

    meet_along_x(barrier)
    meet_heads(barrier)

    @pl.loop(1, nz * CORES)
    def _(place):
        dz, dc = offset(0, place)
        meet(barrier, ahead(0, dz, dc), my_head)

    chosen = index_ref[...].astype(jnp.float32)
    owner_lane = lax.broadcasted_iota(jnp.int32, chosen.shape, 1)
    patch = lax.broadcasted_iota(jnp.int32, (caps, patches), 1).astype(jnp.float32)

    def hits(owner):
        mine = jnp.sum(jnp.where(owner_lane == owner, chosen, 0.0), axis=1, keepdims=True)
        return (mine == patch).astype(jnp.float32)

    @pl.loop(0, nx)
    def _(dx):
        @pl.loop(0, nz, unroll=nz)
        def _(pair):
            dz, _ = offset(dx, pair * CORES)
            both = jnp.concatenate([hits(ahead(dx, dz, 0)), hits(ahead(dx, dz, 1))], axis=0)
            row = pl.multiple_of((dx * nz + pair) * (CORES * caps), CORES * caps)
            pick[pl.ds(row, CORES * caps), :] = both.astype(jnp.bfloat16)

    pl.semaphore_wait(barrier, (nz * CORES - 1) + (nx - 1) + (ny - 1))
    meet_along_x(x_ready)

    half = local_width // CORES
    my_half = pl.ds(pl.multiple_of(my_core * half, half), half)

    def weight_copy(step):
        return pltpu.make_async_remote_copy(
            src_ref=out_weight_ref.at[my_half],
            dst_ref=weight_buf.at[step, my_half],
            send_sem=weight_send_sem.at[step],
            recv_sem=weight_recv_sem.at[step],
            device_id=(me, lax.rem(my_head - step + ny, ny)),
            device_id_type=MESH,
        )

    def pair_copy(step):
        return pltpu.make_async_remote_copy(
            src_ref=weight_buf.at[step, my_half],
            dst_ref=weight_buf.at[step, my_half],
            send_sem=pair_send_sem.at[step],
            recv_sem=pair_recv_sem.at[step],
            device_id=(me + 1 - 2 * my_core, my_head),
            device_id_type=MESH,
        )

    for step in range(1, ny):
        weight_copy(step).start()

    own_queries = pltpu.make_async_copy(
        query_ref.at[pl.ds(pl.multiple_of(me * caps, caps), caps)],
        query_buf.at[0, pl.ds(0, caps)],
        query_recv_sem.at[0],
    )
    own_queries.start()
    def send_queries(place):
        dx, at = lax.div(place, nz * CORES), lax.rem(place, nz * CORES)
        dz, dc = offset(dx, at)
        stripe = behind(dx, dz, dc)
        pltpu.make_async_remote_copy(
            src_ref=query_ref.at[pl.ds(pl.multiple_of(stripe * caps, caps), caps)],
            dst_ref=query_buf.at[dx, pl.ds(pl.multiple_of(at * caps, caps), caps)],
            send_sem=query_send_sem,
            recv_sem=query_recv_sem.at[dx],
            device_id=(stripe, my_head),
            device_id_type=MESH,
        ).start()

    pl.loop(1, nz * CORES)(send_queries)
    if nx > 1:
        pl.semaphore_wait(x_ready, nx - 1)
    meet_heads(heads_ready)
    pl.loop(nz * CORES, peers)(send_queries)

    for copy in weight_copies:
        copy.wait()
    for level in range(levels):
        token_copy(level).wait()

    chunk_slots = nz * CORES * caps

    def project_tokens(dx):
        slots = pl.ds(pl.multiple_of(dx * chunk_slots, chunk_slots), chunk_slots)
        parity = lax.rem(dx, 2)

        def normalize(level):
            raw = jnp.dot(pick[slots, :], token_buf[level], preferred_element_type=jnp.float32)
            shifted = raw - jnp.sum(raw, axis=1, keepdims=True) * (1.0 / width)
            spread = jnp.sum(shifted * shifted, axis=1, keepdims=True) * (1.0 / width)
            return (shifted * lax.rsqrt(spread + 1e-05) * gain_ref[...]).astype(jnp.bfloat16)

        def keep(level, at):
            both = jnp.dot(normed[at], projection[...], preferred_element_type=jnp.float32).astype(jnp.bfloat16)
            keys[parity, level] = both[:, :local_width]
            values[parity, level] = both[:, local_width:]

        normed[0] = normalize(0)

        @pl.loop(0, levels // 2, unroll=levels // 2)
        def _(pair):
            for at in range(2):
                following = normalize(2 * pair + at + 1)
                keep(2 * pair + at, at)
                normed[1 - at] = following

        keep(levels - 1, 0)

    group = CORES * caps
    group_rows = group * latents

    def attend(dx):
        parity = lax.rem(dx, 2)
        whole = query_buf.at[dx]
        pltpu.make_async_copy(whole, whole, query_recv_sem.at[dx]).wait()

        @pl.loop(0, nz, unroll=nz)
        def _(pair):
            slots = pl.ds(pl.multiple_of(pair * group, group), group)
            rows = pl.ds(pl.multiple_of(pair * group_rows, group_rows), group_rows)
            group_keys = keys[parity, :, slots, :].reshape(levels * group, local_width)
            group_values = values[parity, :, slots, :].reshape(levels * group, local_width)
            queries = query_buf[dx, slots].reshape(group_rows, local_width)
            lane_head = lax.broadcasted_iota(jnp.int32, (1, local_width), 1) // HEAD_DIM
            by_head = jnp.concatenate(
                [queries * (lane_head == h).astype(jnp.float32).astype(jnp.bfloat16) for h in range(head_count)],
                axis=0,
            )
            scores = lax.dot_general(
                group_keys, by_head, (((1,), (1,)), ((), ())), preferred_element_type=jnp.float32
            ).reshape(levels, group, head_count * group_rows)
            highest = jnp.max(scores, axis=0, keepdims=True)
            expo = jnp.exp2((scores - highest) * (math.log2(math.e) / math.sqrt(HEAD_DIM)))
            total = jnp.sum(expo, axis=0)
            shape = (group, head_count * group_rows)
            column_slot = (lax.broadcasted_iota(jnp.int32, shape, 1) % group_rows) // latents
            own = lax.broadcasted_iota(jnp.int32, shape, 0) == column_slot
            share_of = jnp.where(own, 1.0 / total, 0.0)
            soft = (expo * share_of[None]).astype(jnp.bfloat16).reshape(levels * group, head_count * group_rows)
            mixed = lax.dot_general(
                soft, group_values, (((0,), (0,)), ((), ())), preferred_element_type=jnp.float32
            )
            result = mixed[:group_rows]
            for h in range(1, head_count):
                result = jnp.where(lane_head == h, mixed[h * group_rows : (h + 1) * group_rows], result)
            mix_send[dx, rows, :] = result.astype(jnp.bfloat16)

        for step in range(1, ny):
            head = lax.rem(my_head - step + ny, ny)
            pltpu.make_async_remote_copy(
                src_ref=mix_send.at[dx, pl.ds(pl.multiple_of(head * share, share), share)],
                dst_ref=mix_recv.at[dx, step - 1],
                send_sem=mix_send_sem,
                recv_sem=mix_recv_sem.at[dx],
                device_id=(me, head),
                device_id_type=MESH,
            ).start()

    def out_copy(dx, place, head):
        dz, dc = offset(dx, my_head * (high * CORES) + place)
        return pltpu.make_async_remote_copy(
            src_ref=out_stage.at[dx, head, pl.ds(pl.multiple_of(place * caps, caps), caps)],
            dst_ref=out_ref.at[pl.ds(pl.multiple_of(me * caps, caps), caps)],
            send_sem=out_send_sem,
            recv_sem=out_recv_sem,
            device_id=(ahead(dx, dz, dc), head),
            device_id_type=MESH,
        )

    def project(dx):
        whole = mix_recv.at[dx]
        pltpu.make_async_copy(whole, whole, mix_recv_sem.at[dx]).wait()
        own = mix_send[dx, pl.ds(pl.multiple_of(my_head * share, share), share), :]
        for head in range(ny):
            columns = slice(head * local_width, (head + 1) * local_width)
            term = jnp.dot(own, weight_buf[0, :, columns], preferred_element_type=jnp.float32)
            summed = term.astype(jnp.bfloat16).astype(jnp.float32)
            for step in range(1, ny):
                term = jnp.dot(
                    mix_recv[dx, step - 1], weight_buf[step, :, columns], preferred_element_type=jnp.float32
                )
                summed += term.astype(jnp.bfloat16).astype(jnp.float32)
            out_stage[dx, head] = summed.astype(jnp.bfloat16).reshape(share // latents, latents, local_width)
        own_place = (dx == 0) & (my_head == 0)

        @pl.when(own_place)
        def _():
            pltpu.make_async_copy(
                out_stage.at[0, 0, pl.ds(0, caps)],
                out_ref.at[pl.ds(pl.multiple_of(me * caps, caps), caps)],
                out_recv_sem,
            ).start()

        @pl.when(jnp.logical_not(own_place))
        def _():
            out_copy(dx, 0, 0).start()

        @pl.loop(1, high * CORES * ny)
        def _(step):
            out_copy(dx, lax.div(step, ny), lax.rem(step, ny)).start()

    @pl.loop(0, nx + 1)
    def _(step):
        @pl.when(step < nx)
        def _():
            project_tokens(step)

        @pl.when(step >= 1)
        def _():
            attend(step - 1)

        @pl.when(step == 1)
        def _():
            own_weight.wait()
            for other in range(1, ny):
                weight_copy(other).wait_recv()
                pair_copy(other).start()

        @pl.when(step == 2)
        def _():
            pl.semaphore_wait(heads_ready, ny - 1)
            for other in range(1, ny):
                pair_copy(other).wait_recv()

        @pl.when(step >= 2)
        def _():
            project(step - 2)

    if nx == 1:
        pl.semaphore_wait(heads_ready, ny - 1)
        for other in range(1, ny):
            pair_copy(other).wait_recv()
    project(nx - 1)

    def drain(ref, sem):
        pltpu.make_async_copy(ref, ref, sem).wait()

    drain(query_ref.at[pl.ds(0, (peers - 1) * caps)], query_send_sem)
    for step in range(1, ny):
        weight_copy(step).wait_send()
        pair_copy(step).wait_send()
    drain(mix_send.at[:, pl.ds(0, (ny - 1) * share)], mix_send_sem)
    drain(out_ref.at[pl.ds(0, (peers - 1) * caps)], out_send_sem)

    @pl.when(my_head != 0)
    def _():
        drain(out_ref.at[pl.ds(0, caps)], out_send_sem)

    drain(out_ref, out_recv_sem)


def shards(sizes, level_tokens, ln_gain, key_weight, value_weight, out_weight, ocean_queries, send_slots):
    nx, nz, ny = sizes
    patches, levels, width = level_tokens.shape
    slot_count, latents, local_width = ocean_queries.shape
    caps = send_slots.shape[2]
    block = caps * latents
    share = nz // ny * CORES * block
    chunk = nz * CORES * block
    vmem = pl.BlockSpec(memory_space=pltpu.VMEM)
    anywhere = pl.BlockSpec(memory_space=pl.ANY)
    stay = pl.BlockSpec(memory_space=pltpu.HBM)
    bf16 = jnp.bfloat16
    dma = pltpu.SemaphoreType.DMA
    return pl.pallas_call(
        functools.partial(attend_kernel, (nx, nz, ny, caps, latents)),
        out_shape=jax.ShapeDtypeStruct((slot_count, latents, local_width), bf16),
        in_specs=[vmem, stay, vmem, stay, stay, stay, anywhere],
        out_specs=anywhere,
        scratch_shapes=[
            pltpu.VMEM((levels, patches, width), bf16),
            pltpu.VMEM((width, 2 * local_width), bf16),
            pltpu.VMEM((2, slot_count // nx, width), bf16),
            pltpu.VMEM((slot_count, patches), bf16),
            pltpu.VMEM((2, levels, slot_count // nx, local_width), bf16),
            pltpu.VMEM((2, levels, slot_count // nx, local_width), bf16),
            pltpu.VMEM((nx, chunk // latents, latents, local_width), bf16),
            pltpu.VMEM((nx, chunk, local_width), bf16),
            pltpu.VMEM((nx, ny - 1, share, local_width), bf16),
            pltpu.VMEM((ny, local_width, width), bf16),
            pltpu.VMEM((nx, ny, share // latents, latents, local_width), bf16),
            dma((levels,)),
            dma((2,)),
            dma,
            dma((nx,)),
            dma,
            dma((nx,)),
            dma((ny,)),
            dma((ny,)),
            dma((ny,)),
            dma((ny,)),
            dma,
            dma,
            pltpu.SemaphoreType.REGULAR,
            pltpu.SemaphoreType.REGULAR,
        ],
        compiler_params=pltpu.CompilerParams(
            collective_id=0, has_side_effects=True, vmem_limit_bytes=60 * 1024 * 1024
        ),
    )(
        send_slots.reshape(-1, caps).T,
        level_tokens.transpose(1, 0, 2),
        ln_gain.reshape(1, width),
        key_weight,
        value_weight,
        out_weight,
        ocean_queries,
    )


def solution(mesh):
    ny = mesh.shape["head"]
    nz = 2 * ny
    nx = mesh.shape["lat"] // (nz * CORES)
    return jax.shard_map(
        functools.partial(shards, (nx, nz, ny)),
        mesh=mesh,
        in_specs=(
            P("lat", None, None),
            P(),
            P(None, "head"),
            P(None, "head"),
            P("head", None),
            P("lat", None, "head"),
            P("lat", None, None),
        ),
        out_specs=P("lat", None, "head"),
        check_vma=False,
    )
```

```python
import functools
import math

import jax
import jax.numpy as jnp
from jax import lax
from jax.experimental import pallas as pl
from jax.experimental.pallas import tpu as pltpu
from jax.sharding import PartitionSpec as P

HEAD_DIM = 64
CORES = 2
MESH = pl.DeviceIdType.MESH


def attend_kernel(
    dims,
    index_ref,
    token_ref,
    gain_ref,
    key_weight_ref,
    value_weight_ref,
    out_weight_ref,
    query_ref,
    out_ref,
    token_buf,
    projection,
    normed,
    pick,
    keys,
    values,
    query_buf,
    mix_send,
    mix_recv,
    weight_buf,
    out_stage,
    token_sem,
    projection_sem,
    query_send_sem,
    query_recv_sem,
    mix_send_sem,
    mix_recv_sem,
    weight_send_sem,
    weight_recv_sem,
    pair_send_sem,
    pair_recv_sem,
    out_send_sem,
    out_recv_sem,
    x_ready,
    heads_ready,
):
    nx, nz, ny, caps, latents = dims
    levels, patches, width = token_ref.shape
    local_width = key_weight_ref.shape[1]
    head_count = local_width // HEAD_DIM
    peers = nx * nz * CORES
    high = nz // ny
    block = caps * latents
    share = high * CORES * block
    chunk = nz * CORES * block
    me, my_head = lax.axis_index("lat"), lax.axis_index("head")
    my_x = lax.div(me, nz * CORES)
    my_z = lax.rem(lax.div(me, CORES), nz)
    my_core = lax.rem(me, CORES)

    def offset(place):
        head, at = lax.div(place, high * CORES), lax.rem(place, high * CORES)
        return (ny // CORES) * at + lax.div(head, CORES), lax.rem(head, CORES)

    def ahead(dx, dz, dc):
        return (lax.rem(my_x + dx, nx) * nz + lax.rem(my_z + dz, nz)) * CORES + lax.rem(my_core + dc, CORES)

    def behind(dx, dz, dc):
        return (lax.rem(my_x - dx + nx, nx) * nz + lax.rem(my_z - dz + nz, nz)) * CORES + lax.rem(
            my_core + dc, CORES
        )

    def token_copy(level):
        return pltpu.make_async_copy(token_ref.at[level], token_buf.at[level], token_sem.at[level])

    weight_copies = [
        pltpu.make_async_copy(ref, projection.at[:, pl.ds(at * local_width, local_width)], projection_sem.at[at])
        for at, ref in enumerate((key_weight_ref, value_weight_ref))
    ]
    own_weight = pltpu.make_async_copy(out_weight_ref, weight_buf.at[0], weight_recv_sem.at[0])
    for level in range(levels):
        token_copy(level).start()
    for copy in weight_copies:
        copy.start()
    own_weight.start()

    barrier = pltpu.get_barrier_semaphore()

    def meet(semaphore, lat, head):
        pl.semaphore_signal(semaphore, inc=1, device_id=(lat, head), device_id_type=MESH)

    def meet_along_x(semaphore):
        for dx in range(1, nx):
            meet(semaphore, ahead(dx, 0, 0), my_head)

    def meet_heads(semaphore):
        for step in range(1, ny):
            meet(semaphore, me, lax.rem(my_head + step, ny))

    meet_along_x(barrier)
    meet_heads(barrier)

    @pl.loop(1, nz * CORES)
    def _(place):
        dz, dc = offset(place)
        meet(barrier, ahead(0, dz, dc), my_head)

    chosen = index_ref[...].astype(jnp.float32)
    owner_lane = lax.broadcasted_iota(jnp.int32, chosen.shape, 1)
    patch = lax.broadcasted_iota(jnp.int32, (caps, patches), 1).astype(jnp.float32)

    def hits(owner):
        mine = jnp.sum(jnp.where(owner_lane == owner, chosen, 0.0), axis=1, keepdims=True)
        return (mine == patch).astype(jnp.float32)

    @pl.loop(0, nx)
    def _(dx):
        @pl.loop(0, nz, unroll=nz)
        def _(pair):
            both = jnp.concatenate(
                [hits(ahead(dx, *offset(pair * CORES))), hits(ahead(dx, *offset(pair * CORES + 1)))], axis=0
            )
            row = pl.multiple_of((dx * nz + pair) * (CORES * caps), CORES * caps)
            pick[pl.ds(row, CORES * caps), :] = both.astype(jnp.bfloat16)

    pl.semaphore_wait(barrier, (nz * CORES - 1) + (nx - 1) + (ny - 1))
    meet_along_x(x_ready)

    half = local_width // CORES
    my_half = pl.ds(pl.multiple_of(my_core * half, half), half)

    def weight_copy(step):
        return pltpu.make_async_remote_copy(
            src_ref=out_weight_ref.at[my_half],
            dst_ref=weight_buf.at[step, my_half],
            send_sem=weight_send_sem.at[step],
            recv_sem=weight_recv_sem.at[step],
            device_id=(me, lax.rem(my_head - step + ny, ny)),
            device_id_type=MESH,
        )

    def pair_copy(step):
        return pltpu.make_async_remote_copy(
            src_ref=weight_buf.at[step, my_half],
            dst_ref=weight_buf.at[step, my_half],
            send_sem=pair_send_sem.at[step],
            recv_sem=pair_recv_sem.at[step],
            device_id=(me + 1 - 2 * my_core, my_head),
            device_id_type=MESH,
        )

    for step in range(1, ny):
        weight_copy(step).start()

    own_queries = pltpu.make_async_copy(
        query_ref.at[pl.ds(pl.multiple_of(me * caps, caps), caps)],
        query_buf.at[0, pl.ds(0, caps)],
        query_recv_sem.at[0],
    )
    own_queries.start()
    def send_queries(place):
        dx, at = lax.div(place, nz * CORES), lax.rem(place, nz * CORES)
        dz, dc = offset(at)
        stripe = behind(dx, dz, dc)
        pltpu.make_async_remote_copy(
            src_ref=query_ref.at[pl.ds(pl.multiple_of(stripe * caps, caps), caps)],
            dst_ref=query_buf.at[dx, pl.ds(pl.multiple_of(at * caps, caps), caps)],
            send_sem=query_send_sem,
            recv_sem=query_recv_sem.at[dx],
            device_id=(stripe, my_head),
            device_id_type=MESH,
        ).start()

    pl.loop(1, nz * CORES)(send_queries)
    if nx > 1:
        pl.semaphore_wait(x_ready, nx - 1)
    meet_heads(heads_ready)
    pl.loop(nz * CORES, peers)(send_queries)

    for copy in weight_copies:
        copy.wait()
    for level in range(levels):
        token_copy(level).wait()

    chunk_slots = nz * CORES * caps

    def project_tokens(dx):
        slots = pl.ds(pl.multiple_of(dx * chunk_slots, chunk_slots), chunk_slots)
        parity = lax.rem(dx, 2)

        def normalize(level):
            raw = jnp.dot(pick[slots, :], token_buf[level], preferred_element_type=jnp.float32)
            shifted = raw - jnp.sum(raw, axis=1, keepdims=True) * (1.0 / width)
            spread = jnp.sum(shifted * shifted, axis=1, keepdims=True) * (1.0 / width)
            return (shifted * lax.rsqrt(spread + 1e-05) * gain_ref[...]).astype(jnp.bfloat16)

        def keep(level, at):
            both = jnp.dot(normed[at], projection[...], preferred_element_type=jnp.float32).astype(jnp.bfloat16)
            keys[parity, level] = both[:, :local_width]
            values[parity, level] = both[:, local_width:]

        normed[0] = normalize(0)

        @pl.loop(0, levels // 2, unroll=levels // 2)
        def _(pair):
            for at in range(2):
                following = normalize(2 * pair + at + 1)
                keep(2 * pair + at, at)
                normed[1 - at] = following

        keep(levels - 1, 0)

    group = CORES * caps
    group_rows = group * latents

    def attend(dx):
        parity = lax.rem(dx, 2)
        whole = query_buf.at[dx]
        pltpu.make_async_copy(whole, whole, query_recv_sem.at[dx]).wait()

        @pl.loop(0, nz, unroll=nz)
        def _(pair):
            slots = pl.ds(pl.multiple_of(pair * group, group), group)
            rows = pl.ds(pl.multiple_of(pair * group_rows, group_rows), group_rows)
            group_keys = keys[parity, :, slots, :].reshape(levels * group, local_width)
            group_values = values[parity, :, slots, :].reshape(levels * group, local_width)
            queries = query_buf[dx, slots].reshape(group_rows, local_width)
            lane_head = lax.broadcasted_iota(jnp.int32, (1, local_width), 1) // HEAD_DIM
            by_head = jnp.concatenate(
                [queries * (lane_head == h).astype(jnp.float32).astype(jnp.bfloat16) for h in range(head_count)],
                axis=0,
            )
            scores = lax.dot_general(
                group_keys, by_head, (((1,), (1,)), ((), ())), preferred_element_type=jnp.float32
            ).reshape(levels, group, head_count * group_rows)
            highest = jnp.max(scores, axis=0, keepdims=True)
            expo = jnp.exp2((scores - highest) * (math.log2(math.e) / math.sqrt(HEAD_DIM)))
            total = jnp.sum(expo, axis=0)
            shape = (group, head_count * group_rows)
            column_slot = (lax.broadcasted_iota(jnp.int32, shape, 1) % group_rows) // latents
            own = lax.broadcasted_iota(jnp.int32, shape, 0) == column_slot
            share_of = jnp.where(own, 1.0 / total, 0.0)
            soft = (expo * share_of[None]).astype(jnp.bfloat16).reshape(levels * group, head_count * group_rows)
            mixed = lax.dot_general(
                soft, group_values, (((0,), (0,)), ((), ())), preferred_element_type=jnp.float32
            )
            result = mixed[:group_rows]
            for h in range(1, head_count):
                result = jnp.where(lane_head == h, mixed[h * group_rows : (h + 1) * group_rows], result)
            mix_send[dx, rows, :] = result.astype(jnp.bfloat16)

        for step in range(1, ny):
            head = lax.rem(my_head - step + ny, ny)
            pltpu.make_async_remote_copy(
                src_ref=mix_send.at[dx, pl.ds(pl.multiple_of(head * share, share), share)],
                dst_ref=mix_recv.at[dx, step - 1],
                send_sem=mix_send_sem,
                recv_sem=mix_recv_sem.at[dx],
                device_id=(me, head),
                device_id_type=MESH,
            ).start()

    def out_copy(dx, place, head):
        dz, dc = offset(my_head * (high * CORES) + place)
        return pltpu.make_async_remote_copy(
            src_ref=out_stage.at[dx, head, pl.ds(pl.multiple_of(place * caps, caps), caps)],
            dst_ref=out_ref.at[pl.ds(pl.multiple_of(me * caps, caps), caps)],
            send_sem=out_send_sem,
            recv_sem=out_recv_sem,
            device_id=(ahead(dx, dz, dc), head),
            device_id_type=MESH,
        )

    def project(dx):
        whole = mix_recv.at[dx]
        pltpu.make_async_copy(whole, whole, mix_recv_sem.at[dx]).wait()
        own = mix_send[dx, pl.ds(pl.multiple_of(my_head * share, share), share), :]
        for head in range(ny):
            columns = slice(head * local_width, (head + 1) * local_width)
            term = jnp.dot(own, weight_buf[0, :, columns], preferred_element_type=jnp.float32)
            summed = term.astype(jnp.bfloat16).astype(jnp.float32)
            for step in range(1, ny):
                term = jnp.dot(
                    mix_recv[dx, step - 1], weight_buf[step, :, columns], preferred_element_type=jnp.float32
                )
                summed += term.astype(jnp.bfloat16).astype(jnp.float32)
            out_stage[dx, head] = summed.astype(jnp.bfloat16).reshape(share // latents, latents, local_width)
        own_place = (dx == 0) & (my_head == 0)

        @pl.when(own_place)
        def _():
            pltpu.make_async_copy(
                out_stage.at[0, 0, pl.ds(0, caps)],
                out_ref.at[pl.ds(pl.multiple_of(me * caps, caps), caps)],
                out_recv_sem,
            ).start()

        @pl.when(jnp.logical_not(own_place))
        def _():
            out_copy(dx, 0, 0).start()

        @pl.loop(1, high * CORES * ny)
        def _(step):
            out_copy(dx, lax.div(step, ny), lax.rem(step, ny)).start()

    @pl.loop(0, nx + 1)
    def _(step):
        @pl.when(step < nx)
        def _():
            project_tokens(step)

        @pl.when(step >= 1)
        def _():
            attend(step - 1)

        @pl.when(step == 1)
        def _():
            own_weight.wait()
            for other in range(1, ny):
                weight_copy(other).wait_recv()
                pair_copy(other).start()

        @pl.when(step == 2)
        def _():
            pl.semaphore_wait(heads_ready, ny - 1)
            for other in range(1, ny):
                pair_copy(other).wait_recv()

        @pl.when(step >= 2)
        def _():
            project(step - 2)

    if nx == 1:
        pl.semaphore_wait(heads_ready, ny - 1)
        for other in range(1, ny):
            pair_copy(other).wait_recv()
    project(nx - 1)

    def drain(ref, sem):
        pltpu.make_async_copy(ref, ref, sem).wait()

    drain(query_ref.at[pl.ds(0, (peers - 1) * caps)], query_send_sem)
    for step in range(1, ny):
        weight_copy(step).wait_send()
        pair_copy(step).wait_send()
    drain(mix_send.at[:, pl.ds(0, (ny - 1) * share)], mix_send_sem)
    drain(out_ref.at[pl.ds(0, (peers - 1) * caps)], out_send_sem)

    @pl.when(my_head != 0)
    def _():
        drain(out_ref.at[pl.ds(0, caps)], out_send_sem)

    drain(out_ref, out_recv_sem)


def shards(sizes, level_tokens, ln_gain, key_weight, value_weight, out_weight, ocean_queries, send_slots):
    nx, nz, ny = sizes
    patches, levels, width = level_tokens.shape
    slot_count, latents, local_width = ocean_queries.shape
    caps = send_slots.shape[2]
    block = caps * latents
    share = nz // ny * CORES * block
    chunk = nz * CORES * block
    vmem = pl.BlockSpec(memory_space=pltpu.VMEM)
    anywhere = pl.BlockSpec(memory_space=pl.ANY)
    stay = pl.BlockSpec(memory_space=pltpu.HBM)
    bf16 = jnp.bfloat16
    dma = pltpu.SemaphoreType.DMA
    return pl.pallas_call(
        functools.partial(attend_kernel, (nx, nz, ny, caps, latents)),
        out_shape=jax.ShapeDtypeStruct((slot_count, latents, local_width), bf16),
        in_specs=[vmem, stay, vmem, stay, stay, stay, anywhere],
        out_specs=anywhere,
        scratch_shapes=[
            pltpu.VMEM((levels, patches, width), bf16),
            pltpu.VMEM((width, 2 * local_width), bf16),
            pltpu.VMEM((2, slot_count // nx, width), bf16),
            pltpu.VMEM((slot_count, patches), bf16),
            pltpu.VMEM((2, levels, slot_count // nx, local_width), bf16),
            pltpu.VMEM((2, levels, slot_count // nx, local_width), bf16),
            pltpu.VMEM((nx, chunk // latents, latents, local_width), bf16),
            pltpu.VMEM((nx, chunk, local_width), bf16),
            pltpu.VMEM((nx, ny - 1, share, local_width), bf16),
            pltpu.VMEM((ny, local_width, width), bf16),
            pltpu.VMEM((nx, ny, share // latents, latents, local_width), bf16),
            dma((levels,)),
            dma((2,)),
            dma,
            dma((nx,)),
            dma,
            dma((nx,)),
            dma((ny,)),
            dma((ny,)),
            dma((ny,)),
            dma((ny,)),
            dma,
            dma,
            pltpu.SemaphoreType.REGULAR,
            pltpu.SemaphoreType.REGULAR,
        ],
        compiler_params=pltpu.CompilerParams(
            collective_id=0, has_side_effects=True, vmem_limit_bytes=60 * 1024 * 1024
        ),
    )(
        send_slots.reshape(-1, caps).T,
        level_tokens.transpose(1, 0, 2),
        ln_gain.reshape(1, width),
        key_weight,
        value_weight,
        out_weight,
        ocean_queries,
    )


def solution(mesh):
    ny = mesh.shape["head"]
    nz = 2 * ny
    nx = mesh.shape["lat"] // (nz * CORES)
    return jax.shard_map(
        functools.partial(shards, (nx, nz, ny)),
        mesh=mesh,
        in_specs=(
            P("lat", None, None),
            P(),
            P(None, "head"),
            P(None, "head"),
            P("head", None),
            P("lat", None, "head"),
            P("lat", None, None),
        ),
        out_specs=P("lat", None, "head"),
        check_vma=False,
    )
```

```python
import functools
import math

import jax
import jax.numpy as jnp
from jax import lax
from jax.experimental import pallas as pl
from jax.experimental.pallas import tpu as pltpu
from jax.sharding import PartitionSpec as P

HEAD_DIM = 64
CORES = 2
MESH = pl.DeviceIdType.MESH


def attend_kernel(
    dims,
    index_ref,
    token_ref,
    gain_ref,
    key_weight_ref,
    value_weight_ref,
    out_weight_ref,
    query_ref,
    out_ref,
    token_buf,
    projection,
    normed,
    pick,
    keys,
    values,
    query_buf,
    mix_send,
    mix_recv,
    weight_buf,
    out_stage,
    token_sem,
    projection_sem,
    query_send_sem,
    query_recv_sem,
    mix_send_sem,
    mix_recv_sem,
    weight_send_sem,
    weight_recv_sem,
    pair_send_sem,
    pair_recv_sem,
    out_send_sem,
    out_recv_sem,
    x_ready,
    heads_ready,
):
    nx, nz, ny, caps, latents = dims
    levels, patches, width = token_ref.shape
    local_width = key_weight_ref.shape[1]
    head_count = local_width // HEAD_DIM
    peers = nx * nz * CORES
    high = nz // ny
    block = caps * latents
    share = high * CORES * block
    chunk = nz * CORES * block
    me, my_head = lax.axis_index("lat"), lax.axis_index("head")
    my_x = lax.div(me, nz * CORES)
    my_z = lax.rem(lax.div(me, CORES), nz)
    my_core = lax.rem(me, CORES)

    def offset(place):
        head, at = lax.div(place, high * CORES), lax.rem(place, high * CORES)
        return (ny // CORES) * at + lax.div(head, CORES), lax.rem(head, CORES)

    def ahead(dx, dz, dc):
        return (lax.rem(my_x + dx, nx) * nz + lax.rem(my_z + dz, nz)) * CORES + lax.rem(my_core + dc, CORES)

    def behind(dx, dz, dc):
        return (lax.rem(my_x - dx + nx, nx) * nz + lax.rem(my_z - dz + nz, nz)) * CORES + lax.rem(
            my_core + dc, CORES
        )

    def token_copy(level):
        return pltpu.make_async_copy(token_ref.at[level], token_buf.at[level], token_sem.at[level])

    weight_copies = [
        pltpu.make_async_copy(ref, projection.at[:, pl.ds(at * local_width, local_width)], projection_sem.at[at])
        for at, ref in enumerate((key_weight_ref, value_weight_ref))
    ]
    own_weight = pltpu.make_async_copy(out_weight_ref, weight_buf.at[0], weight_recv_sem.at[0])
    for level in range(levels):
        token_copy(level).start()
    for copy in weight_copies:
        copy.start()
    own_weight.start()

    barrier = pltpu.get_barrier_semaphore()

    def meet(semaphore, lat, head):
        pl.semaphore_signal(semaphore, inc=1, device_id=(lat, head), device_id_type=MESH)

    def meet_along_x(semaphore):
        for dx in range(1, nx):
            meet(semaphore, ahead(dx, 0, 0), my_head)

    def meet_heads(semaphore):
        for step in range(1, ny):
            meet(semaphore, me, lax.rem(my_head + step, ny))

    meet_along_x(barrier)
    meet_heads(barrier)

    @pl.loop(1, nz * CORES)
    def _(place):
        dz, dc = offset(place)
        meet(barrier, ahead(0, dz, dc), my_head)

    pl.semaphore_wait(barrier, (nz * CORES - 1) + (nx - 1) + (ny - 1))
    meet_along_x(x_ready)

    half = local_width // CORES
    my_half = pl.ds(pl.multiple_of(my_core * half, half), half)

    def weight_copy(step):
        return pltpu.make_async_remote_copy(
            src_ref=out_weight_ref.at[my_half],
            dst_ref=weight_buf.at[step, my_half],
            send_sem=weight_send_sem.at[step],
            recv_sem=weight_recv_sem.at[step],
            device_id=(me, lax.rem(my_head - step + ny, ny)),
            device_id_type=MESH,
        )

    def pair_copy(step):
        return pltpu.make_async_remote_copy(
            src_ref=weight_buf.at[step, my_half],
            dst_ref=weight_buf.at[step, my_half],
            send_sem=pair_send_sem.at[step],
            recv_sem=pair_recv_sem.at[step],
            device_id=(me + 1 - 2 * my_core, my_head),
            device_id_type=MESH,
        )

    own_queries = pltpu.make_async_copy(
        query_ref.at[pl.ds(pl.multiple_of(me * caps, caps), caps)],
        query_buf.at[0, pl.ds(0, caps)],
        query_recv_sem.at[0],
    )
    own_queries.start()
    def send_queries(place):
        dx, at = lax.div(place, nz * CORES), lax.rem(place, nz * CORES)
        dz, dc = offset(at)
        stripe = behind(dx, dz, dc)
        pltpu.make_async_remote_copy(
            src_ref=query_ref.at[pl.ds(pl.multiple_of(stripe * caps, caps), caps)],
            dst_ref=query_buf.at[dx, pl.ds(pl.multiple_of(at * caps, caps), caps)],
            send_sem=query_send_sem,
            recv_sem=query_recv_sem.at[dx],
            device_id=(stripe, my_head),
            device_id_type=MESH,
        ).start()

    pl.loop(1, nz * CORES)(send_queries)
    for step in range(1, ny):
        weight_copy(step).start()

    if nx > 1:
        pl.semaphore_wait(x_ready, nx - 1)
    meet_heads(heads_ready)
    pl.loop(nz * CORES, peers)(send_queries)

    chosen = index_ref[...].astype(jnp.float32)
    owner_lane = lax.broadcasted_iota(jnp.int32, chosen.shape, 1)
    patch = lax.broadcasted_iota(jnp.int32, (caps, patches), 1).astype(jnp.float32)

    def hits(owner):
        mine = jnp.sum(jnp.where(owner_lane == owner, chosen, 0.0), axis=1, keepdims=True)
        return (mine == patch).astype(jnp.float32)

    @pl.loop(0, nx)
    def _(dx):
        @pl.loop(0, nz, unroll=nz)
        def _(pair):
            both = jnp.concatenate(
                [hits(ahead(dx, *offset(pair * CORES))), hits(ahead(dx, *offset(pair * CORES + 1)))], axis=0
            )
            row = pl.multiple_of((dx * nz + pair) * (CORES * caps), CORES * caps)
            pick[pl.ds(row, CORES * caps), :] = both.astype(jnp.bfloat16)

    for copy in weight_copies:
        copy.wait()
    for level in range(levels):
        token_copy(level).wait()

    chunk_slots = nz * CORES * caps

    def project_tokens(dx):
        slots = pl.ds(pl.multiple_of(dx * chunk_slots, chunk_slots), chunk_slots)
        parity = lax.rem(dx, 2)

        def normalize(level):
            raw = jnp.dot(pick[slots, :], token_buf[level], preferred_element_type=jnp.float32)
            shifted = raw - jnp.sum(raw, axis=1, keepdims=True) * (1.0 / width)
            spread = jnp.sum(shifted * shifted, axis=1, keepdims=True) * (1.0 / width)
            return (shifted * lax.rsqrt(spread + 1e-05) * gain_ref[...]).astype(jnp.bfloat16)

        def keep(level, at):
            both = jnp.dot(normed[at], projection[...], preferred_element_type=jnp.float32).astype(jnp.bfloat16)
            keys[parity, level] = both[:, :local_width]
            values[parity, level] = both[:, local_width:]

        normed[0] = normalize(0)

        @pl.loop(0, levels // 2, unroll=levels // 2)
        def _(pair):
            for at in range(2):
                following = normalize(2 * pair + at + 1)
                keep(2 * pair + at, at)
                normed[1 - at] = following

        keep(levels - 1, 0)

    group = CORES * caps
    group_rows = group * latents

    def attend(dx):
        parity = lax.rem(dx, 2)
        whole = query_buf.at[dx]
        pltpu.make_async_copy(whole, whole, query_recv_sem.at[dx]).wait()

        @pl.loop(0, nz, unroll=nz)
        def _(pair):
            slots = pl.ds(pl.multiple_of(pair * group, group), group)
            rows = pl.ds(pl.multiple_of(pair * group_rows, group_rows), group_rows)
            group_keys = keys[parity, :, slots, :].reshape(levels * group, local_width)
            group_values = values[parity, :, slots, :].reshape(levels * group, local_width)
            queries = query_buf[dx, slots].reshape(group_rows, local_width)
            lane_head = lax.broadcasted_iota(jnp.int32, (1, local_width), 1) // HEAD_DIM
            by_head = jnp.concatenate(
                [queries * (lane_head == h).astype(jnp.float32).astype(jnp.bfloat16) for h in range(head_count)],
                axis=0,
            )
            scores = lax.dot_general(
                group_keys, by_head, (((1,), (1,)), ((), ())), preferred_element_type=jnp.float32
            ).reshape(levels, group, head_count * group_rows)
            highest = jnp.max(scores, axis=0, keepdims=True)
            expo = jnp.exp2((scores - highest) * (math.log2(math.e) / math.sqrt(HEAD_DIM)))
            total = jnp.sum(expo, axis=0)
            shape = (group, head_count * group_rows)
            column_slot = (lax.broadcasted_iota(jnp.int32, shape, 1) % group_rows) // latents
            own = lax.broadcasted_iota(jnp.int32, shape, 0) == column_slot
            share_of = jnp.where(own, 1.0 / total, 0.0)
            soft = (expo * share_of[None]).astype(jnp.bfloat16).reshape(levels * group, head_count * group_rows)
            mixed = lax.dot_general(
                soft, group_values, (((0,), (0,)), ((), ())), preferred_element_type=jnp.float32
            )
            result = mixed[:group_rows]
            for h in range(1, head_count):
                result = jnp.where(lane_head == h, mixed[h * group_rows : (h + 1) * group_rows], result)
            mix_send[dx, rows, :] = result.astype(jnp.bfloat16)

        for step in range(1, ny):
            head = lax.rem(my_head - step + ny, ny)
            pltpu.make_async_remote_copy(
                src_ref=mix_send.at[dx, pl.ds(pl.multiple_of(head * share, share), share)],
                dst_ref=mix_recv.at[dx, step - 1],
                send_sem=mix_send_sem,
                recv_sem=mix_recv_sem.at[dx],
                device_id=(me, head),
                device_id_type=MESH,
            ).start()

    def out_copy(dx, place, head):
        dz, dc = offset(my_head * (high * CORES) + place)
        return pltpu.make_async_remote_copy(
            src_ref=out_stage.at[dx, head, pl.ds(pl.multiple_of(place * caps, caps), caps)],
            dst_ref=out_ref.at[pl.ds(pl.multiple_of(me * caps, caps), caps)],
            send_sem=out_send_sem,
            recv_sem=out_recv_sem,
            device_id=(ahead(dx, dz, dc), head),
            device_id_type=MESH,
        )

    def project(dx):
        whole = mix_recv.at[dx]
        pltpu.make_async_copy(whole, whole, mix_recv_sem.at[dx]).wait()
        own = mix_send[dx, pl.ds(pl.multiple_of(my_head * share, share), share), :]
        for head in range(ny):
            columns = slice(head * local_width, (head + 1) * local_width)
            term = jnp.dot(own, weight_buf[0, :, columns], preferred_element_type=jnp.float32)
            summed = term.astype(jnp.bfloat16).astype(jnp.float32)
            for step in range(1, ny):
                term = jnp.dot(
                    mix_recv[dx, step - 1], weight_buf[step, :, columns], preferred_element_type=jnp.float32
                )
                summed += term.astype(jnp.bfloat16).astype(jnp.float32)
            out_stage[dx, head] = summed.astype(jnp.bfloat16).reshape(share // latents, latents, local_width)
        own_place = (dx == 0) & (my_head == 0)

        @pl.when(own_place)
        def _():
            pltpu.make_async_copy(
                out_stage.at[0, 0, pl.ds(0, caps)],
                out_ref.at[pl.ds(pl.multiple_of(me * caps, caps), caps)],
                out_recv_sem,
            ).start()

        @pl.when(jnp.logical_not(own_place))
        def _():
            out_copy(dx, 0, 0).start()

        @pl.loop(1, high * CORES * ny)
        def _(step):
            out_copy(dx, lax.div(step, ny), lax.rem(step, ny)).start()

    @pl.loop(0, nx + 1)
    def _(step):
        @pl.when(step < nx)
        def _():
            project_tokens(step)

        @pl.when(step >= 1)
        def _():
            attend(step - 1)

        @pl.when(step == 1)
        def _():
            own_weight.wait()
            for other in range(1, ny):
                weight_copy(other).wait_recv()
                pair_copy(other).start()

        @pl.when(step == 2)
        def _():
            pl.semaphore_wait(heads_ready, ny - 1)
            for other in range(1, ny):
                pair_copy(other).wait_recv()

        @pl.when(step >= 2)
        def _():
            project(step - 2)

    if nx == 1:
        pl.semaphore_wait(heads_ready, ny - 1)
        for other in range(1, ny):
            pair_copy(other).wait_recv()
    project(nx - 1)

    def drain(ref, sem):
        pltpu.make_async_copy(ref, ref, sem).wait()

    drain(query_ref.at[pl.ds(0, (peers - 1) * caps)], query_send_sem)
    for step in range(1, ny):
        weight_copy(step).wait_send()
        pair_copy(step).wait_send()
    drain(mix_send.at[:, pl.ds(0, (ny - 1) * share)], mix_send_sem)
    drain(out_ref.at[pl.ds(0, (peers - 1) * caps)], out_send_sem)

    @pl.when(my_head != 0)
    def _():
        drain(out_ref.at[pl.ds(0, caps)], out_send_sem)

    drain(out_ref, out_recv_sem)


def shards(sizes, level_tokens, ln_gain, key_weight, value_weight, out_weight, ocean_queries, send_slots):
    nx, nz, ny = sizes
    patches, levels, width = level_tokens.shape
    slot_count, latents, local_width = ocean_queries.shape
    caps = send_slots.shape[2]
    block = caps * latents
    share = nz // ny * CORES * block
    chunk = nz * CORES * block
    vmem = pl.BlockSpec(memory_space=pltpu.VMEM)
    anywhere = pl.BlockSpec(memory_space=pl.ANY)
    stay = pl.BlockSpec(memory_space=pltpu.HBM)
    bf16 = jnp.bfloat16
    dma = pltpu.SemaphoreType.DMA
    return pl.pallas_call(
        functools.partial(attend_kernel, (nx, nz, ny, caps, latents)),
        out_shape=jax.ShapeDtypeStruct((slot_count, latents, local_width), bf16),
        in_specs=[vmem, stay, vmem, stay, stay, stay, anywhere],
        out_specs=anywhere,
        scratch_shapes=[
            pltpu.VMEM((levels, patches, width), bf16),
            pltpu.VMEM((width, 2 * local_width), bf16),
            pltpu.VMEM((2, slot_count // nx, width), bf16),
            pltpu.VMEM((slot_count, patches), bf16),
            pltpu.VMEM((2, levels, slot_count // nx, local_width), bf16),
            pltpu.VMEM((2, levels, slot_count // nx, local_width), bf16),
            pltpu.VMEM((nx, chunk // latents, latents, local_width), bf16),
            pltpu.VMEM((nx, chunk, local_width), bf16),
            pltpu.VMEM((nx, ny - 1, share, local_width), bf16),
            pltpu.VMEM((ny, local_width, width), bf16),
            pltpu.VMEM((nx, ny, share // latents, latents, local_width), bf16),
            dma((levels,)),
            dma((2,)),
            dma,
            dma((nx,)),
            dma,
            dma((nx,)),
            dma((ny,)),
            dma((ny,)),
            dma((ny,)),
            dma((ny,)),
            dma,
            dma,
            pltpu.SemaphoreType.REGULAR,
            pltpu.SemaphoreType.REGULAR,
        ],
        compiler_params=pltpu.CompilerParams(
            collective_id=0, has_side_effects=True, vmem_limit_bytes=60 * 1024 * 1024
        ),
    )(
        send_slots.reshape(-1, caps).T,
        level_tokens.transpose(1, 0, 2),
        ln_gain.reshape(1, width),
        key_weight,
        value_weight,
        out_weight,
        ocean_queries,
    )


def solution(mesh):
    ny = mesh.shape["head"]
    nz = 2 * ny
    nx = mesh.shape["lat"] // (nz * CORES)
    return jax.shard_map(
        functools.partial(shards, (nx, nz, ny)),
        mesh=mesh,
        in_specs=(
            P("lat", None, None),
            P(),
            P(None, "head"),
            P(None, "head"),
            P("head", None),
            P("lat", None, "head"),
            P("lat", None, None),
        ),
        out_specs=P("lat", None, "head"),
        check_vma=False,
    )
```

```python
import functools
import math

import jax
import jax.numpy as jnp
from jax import lax
from jax.experimental import pallas as pl
from jax.experimental.pallas import tpu as pltpu
from jax.sharding import PartitionSpec as P

HEAD_DIM = 64
CORES = 2
PIECES = 8
MESH = pl.DeviceIdType.MESH


def attend_kernel(
    dims,
    index_ref,
    token_ref,
    gain_ref,
    key_weight_ref,
    value_weight_ref,
    out_weight_ref,
    query_ref,
    out_ref,
    token_buf,
    projection,
    normed,
    pick,
    keys,
    values,
    query_buf,
    mix_send,
    mix_recv,
    weight_buf,
    out_stage,
    token_sem,
    projection_sem,
    query_send_sem,
    query_recv_sem,
    mix_send_sem,
    mix_recv_sem,
    weight_send_sem,
    weight_recv_sem,
    pair_send_sem,
    pair_recv_sem,
    out_send_sem,
    out_recv_sem,
    x_ready,
    heads_ready,
):
    nx, nz, ny, caps, latents = dims
    levels, patches, width = token_ref.shape
    local_width = key_weight_ref.shape[1]
    head_count = local_width // HEAD_DIM
    peers = nx * nz * CORES
    high = nz // ny
    block = caps * latents
    share = high * CORES * block
    chunk = nz * CORES * block
    me, my_head = lax.axis_index("lat"), lax.axis_index("head")
    my_x = lax.div(me, nz * CORES)
    my_z = lax.rem(lax.div(me, CORES), nz)
    my_core = lax.rem(me, CORES)

    def offset(place):
        head, at = lax.div(place, high * CORES), lax.rem(place, high * CORES)
        return (ny // CORES) * at + lax.div(head, CORES), lax.rem(head, CORES)

    def ahead(dx, dz, dc):
        return (lax.rem(my_x + dx, nx) * nz + lax.rem(my_z + dz, nz)) * CORES + lax.rem(my_core + dc, CORES)

    def behind(dx, dz, dc):
        return (lax.rem(my_x - dx + nx, nx) * nz + lax.rem(my_z - dz + nz, nz)) * CORES + lax.rem(
            my_core + dc, CORES
        )

    def token_copy(level):
        return pltpu.make_async_copy(token_ref.at[level], token_buf.at[level], token_sem.at[level])

    weight_copies = [
        pltpu.make_async_copy(ref, projection.at[:, pl.ds(at * local_width, local_width)], projection_sem.at[at])
        for at, ref in enumerate((key_weight_ref, value_weight_ref))
    ]
    own_weight = pltpu.make_async_copy(out_weight_ref, weight_buf.at[0], weight_recv_sem.at[0])
    for level in range(levels):
        token_copy(level).start()
    for copy in weight_copies:
        copy.start()
    own_weight.start()

    barrier = pltpu.get_barrier_semaphore()

    def meet(semaphore, lat, head):
        pl.semaphore_signal(semaphore, inc=1, device_id=(lat, head), device_id_type=MESH)

    def meet_along_x(semaphore):
        for dx in range(1, nx):
            meet(semaphore, ahead(dx, 0, 0), my_head)

    def meet_heads(semaphore):
        for step in range(1, ny):
            meet(semaphore, me, lax.rem(my_head + step, ny))

    meet_along_x(barrier)
    meet_heads(barrier)

    @pl.loop(1, nz * CORES)
    def _(place):
        dz, dc = offset(place)
        meet(barrier, ahead(0, dz, dc), my_head)

    pl.semaphore_wait(barrier, (nz * CORES - 1) + (nx - 1) + (ny - 1))
    meet_along_x(x_ready)

    half = local_width // CORES
    my_half = pl.ds(pl.multiple_of(my_core * half, half), half)

    def weight_copy(step):
        return pltpu.make_async_remote_copy(
            src_ref=out_weight_ref.at[my_half],
            dst_ref=weight_buf.at[step, my_half],
            send_sem=weight_send_sem.at[step],
            recv_sem=weight_recv_sem.at[step],
            device_id=(me, lax.rem(my_head - step + ny, ny)),
            device_id_type=MESH,
        )

    def pair_copy(step):
        return pltpu.make_async_remote_copy(
            src_ref=weight_buf.at[step, my_half],
            dst_ref=weight_buf.at[step, my_half],
            send_sem=pair_send_sem.at[step],
            recv_sem=pair_recv_sem.at[step],
            device_id=(me + 1 - 2 * my_core, my_head),
            device_id_type=MESH,
        )

    own_queries = pltpu.make_async_copy(
        query_ref.at[pl.ds(pl.multiple_of(me * caps, caps), caps)],
        query_buf.at[0, pl.ds(0, caps)],
        query_recv_sem.at[0],
    )
    own_queries.start()
    def send_queries(place):
        dx, at = lax.div(place, nz * CORES), lax.rem(place, nz * CORES)
        dz, dc = offset(at)
        stripe = behind(dx, dz, dc)
        pltpu.make_async_remote_copy(
            src_ref=query_ref.at[pl.ds(pl.multiple_of(stripe * caps, caps), caps)],
            dst_ref=query_buf.at[dx, pl.ds(pl.multiple_of(at * caps, caps), caps)],
            send_sem=query_send_sem,
            recv_sem=query_recv_sem.at[dx],
            device_id=(stripe, my_head),
            device_id_type=MESH,
        ).start()

    pl.loop(1, nz * CORES)(send_queries)
    for step in range(1, ny):
        weight_copy(step).start()

    if nx > 1:
        pl.semaphore_wait(x_ready, nx - 1)
    meet_heads(heads_ready)
    pl.loop(nz * CORES, peers)(send_queries)

    chosen = index_ref[...].astype(jnp.float32)
    owner_lane = lax.broadcasted_iota(jnp.int32, chosen.shape, 1)
    patch = lax.broadcasted_iota(jnp.int32, (caps, patches), 1).astype(jnp.float32)

    def hits(owner):
        mine = jnp.sum(jnp.where(owner_lane == owner, chosen, 0.0), axis=1, keepdims=True)
        return (mine == patch).astype(jnp.float32)

    @pl.loop(0, nx)
    def _(dx):
        @pl.loop(0, nz, unroll=nz)
        def _(pair):
            both = jnp.concatenate(
                [hits(ahead(dx, *offset(pair * CORES))), hits(ahead(dx, *offset(pair * CORES + 1)))], axis=0
            )
            row = pl.multiple_of((dx * nz + pair) * (CORES * caps), CORES * caps)
            pick[pl.ds(row, CORES * caps), :] = both.astype(jnp.bfloat16)

    for copy in weight_copies:
        copy.wait()
    for level in range(levels):
        token_copy(level).wait()

    chunk_slots = nz * CORES * caps

    def project_tokens(dx):
        slots = pl.ds(pl.multiple_of(dx * chunk_slots, chunk_slots), chunk_slots)
        parity = lax.rem(dx, 2)

        def normalize(level):
            raw = jnp.dot(pick[slots, :], token_buf[level], preferred_element_type=jnp.float32)
            shifted = raw - jnp.sum(raw, axis=1, keepdims=True) * (1.0 / width)
            spread = jnp.sum(shifted * shifted, axis=1, keepdims=True) * (1.0 / width)
            return (shifted * lax.rsqrt(spread + 1e-05) * gain_ref[...]).astype(jnp.bfloat16)

        def keep(level, at):
            both = jnp.dot(normed[at], projection[...], preferred_element_type=jnp.float32).astype(jnp.bfloat16)
            keys[parity, level] = both[:, :local_width]
            values[parity, level] = both[:, local_width:]

        normed[0] = normalize(0)

        @pl.loop(0, levels // 2, unroll=levels // 2)
        def _(pair):
            for at in range(2):
                following = normalize(2 * pair + at + 1)
                keep(2 * pair + at, at)
                normed[1 - at] = following

        keep(levels - 1, 0)

    group = CORES * caps
    group_rows = group * latents

    def attend(dx):
        parity = lax.rem(dx, 2)
        whole = query_buf.at[dx]
        pltpu.make_async_copy(whole, whole, query_recv_sem.at[dx]).wait()

        @pl.loop(0, nz, unroll=nz)
        def _(pair):
            slots = pl.ds(pl.multiple_of(pair * group, group), group)
            rows = pl.ds(pl.multiple_of(pair * group_rows, group_rows), group_rows)
            group_keys = keys[parity, :, slots, :].reshape(levels * group, local_width)
            group_values = values[parity, :, slots, :].reshape(levels * group, local_width)
            queries = query_buf[dx, slots].reshape(group_rows, local_width)
            lane_head = lax.broadcasted_iota(jnp.int32, (1, local_width), 1) // HEAD_DIM
            by_head = jnp.concatenate(
                [queries * (lane_head == h).astype(jnp.float32).astype(jnp.bfloat16) for h in range(head_count)],
                axis=0,
            )
            scores = lax.dot_general(
                group_keys, by_head, (((1,), (1,)), ((), ())), preferred_element_type=jnp.float32
            ).reshape(levels, group, head_count * group_rows)
            highest = jnp.max(scores, axis=0, keepdims=True)
            expo = jnp.exp2((scores - highest) * (math.log2(math.e) / math.sqrt(HEAD_DIM)))
            total = jnp.sum(expo, axis=0)
            shape = (group, head_count * group_rows)
            column_slot = (lax.broadcasted_iota(jnp.int32, shape, 1) % group_rows) // latents
            own = lax.broadcasted_iota(jnp.int32, shape, 0) == column_slot
            share_of = jnp.where(own, 1.0 / total, 0.0)
            soft = (expo * share_of[None]).astype(jnp.bfloat16).reshape(levels * group, head_count * group_rows)
            mixed = lax.dot_general(
                soft, group_values, (((0,), (0,)), ((), ())), preferred_element_type=jnp.float32
            )
            result = mixed[:group_rows]
            for h in range(1, head_count):
                result = jnp.where(lane_head == h, mixed[h * group_rows : (h + 1) * group_rows], result)
            mix_send[dx, rows, :] = result.astype(jnp.bfloat16)

        for step in range(1, ny):
            head = lax.rem(my_head - step + ny, ny)
            pltpu.make_async_remote_copy(
                src_ref=mix_send.at[dx, pl.ds(pl.multiple_of(head * share, share), share)],
                dst_ref=mix_recv.at[dx, step - 1],
                send_sem=mix_send_sem,
                recv_sem=mix_recv_sem.at[dx],
                device_id=(me, head),
                device_id_type=MESH,
            ).start()

    def out_copy(dx, place, head):
        dz, dc = offset(my_head * (high * CORES) + place)
        return pltpu.make_async_remote_copy(
            src_ref=out_stage.at[dx, head, pl.ds(pl.multiple_of(place * caps, caps), caps)],
            dst_ref=out_ref.at[pl.ds(pl.multiple_of(me * caps, caps), caps)],
            send_sem=out_send_sem,
            recv_sem=out_recv_sem,
            device_id=(ahead(dx, dz, dc), head),
            device_id_type=MESH,
        )

    def project(dx):
        whole = mix_recv.at[dx]
        pltpu.make_async_copy(whole, whole, mix_recv_sem.at[dx]).wait()
        own = mix_send[dx, pl.ds(pl.multiple_of(my_head * share, share), share), :]
        for head in range(ny):
            columns = slice(head * local_width, (head + 1) * local_width)
            term = jnp.dot(own, weight_buf[0, :, columns], preferred_element_type=jnp.float32)
            summed = term.astype(jnp.bfloat16).astype(jnp.float32)
            for step in range(1, ny):
                term = jnp.dot(
                    mix_recv[dx, step - 1], weight_buf[step, :, columns], preferred_element_type=jnp.float32
                )
                summed += term.astype(jnp.bfloat16).astype(jnp.float32)
            out_stage[dx, head] = summed.astype(jnp.bfloat16).reshape(share // latents, latents, local_width)
        own_place = (dx == 0) & (my_head == 0)

        @pl.when(own_place)
        def _():
            pltpu.make_async_copy(
                out_stage.at[0, 0, pl.ds(0, caps)],
                out_ref.at[pl.ds(pl.multiple_of(me * caps, caps), caps)],
                out_recv_sem,
            ).start()

        @pl.when(jnp.logical_not(own_place))
        def _():
            out_copy(dx, 0, 0).start()

        @pl.loop(1, high * CORES * ny)
        def _(step):
            out_copy(dx, lax.div(step, ny), lax.rem(step, ny)).start()

    @pl.loop(0, nx + 1)
    def _(step):
        @pl.when(step < nx)
        def _():
            project_tokens(step)

        @pl.when(step >= 1)
        def _():
            attend(step - 1)

        @pl.when(step == 1)
        def _():
            own_weight.wait()
            for other in range(1, ny):
                weight_copy(other).wait_recv()
                pair_copy(other).start()

        @pl.when(step == 2)
        def _():
            pl.semaphore_wait(heads_ready, ny - 1)
            for other in range(1, ny):
                pair_copy(other).wait_recv()

        @pl.when(step >= 2)
        def _():
            project(step - 2)

    if nx == 1:
        pl.semaphore_wait(heads_ready, ny - 1)
        for other in range(1, ny):
            pair_copy(other).wait_recv()
    project(nx - 1)

    def drain(ref, sem):
        pltpu.make_async_copy(ref, ref, sem).wait()

    drain(query_ref.at[pl.ds(0, (peers - 1) * caps)], query_send_sem)
    for step in range(1, ny):
        weight_copy(step).wait_send()
        pair_copy(step).wait_send()
    drain(mix_send.at[:, pl.ds(0, (ny - 1) * share)], mix_send_sem)
    drain(out_ref.at[pl.ds(0, (peers - 1) * caps)], out_send_sem)

    @pl.when(my_head != 0)
    def _():
        drain(out_ref.at[pl.ds(0, caps)], out_send_sem)

    drain(out_ref, out_recv_sem)


def hand_over_kernel(result_ref, out_ref, held, in_sem, out_sem):
    rows = result_ref.shape[0] // PIECES
    pieces = [pl.ds(at * rows, rows) for at in range(PIECES)]
    arriving = [pltpu.make_async_copy(result_ref.at[p], held.at[p], in_sem.at[at]) for at, p in enumerate(pieces)]
    leaving = [pltpu.make_async_copy(held.at[p], out_ref.at[p], out_sem.at[at]) for at, p in enumerate(pieces)]
    for copy in arriving:
        copy.start()
    for first, second in zip(arriving, leaving):
        first.wait()
        second.start()
    for copy in leaving:
        copy.wait()


def shards(sizes, level_tokens, ln_gain, key_weight, value_weight, out_weight, ocean_queries, send_slots):
    nx, nz, ny = sizes
    patches, levels, width = level_tokens.shape
    slot_count, latents, local_width = ocean_queries.shape
    caps = send_slots.shape[2]
    block = caps * latents
    share = nz // ny * CORES * block
    chunk = nz * CORES * block
    vmem = pl.BlockSpec(memory_space=pltpu.VMEM)
    anywhere = pl.BlockSpec(memory_space=pl.ANY)
    stay = pl.BlockSpec(memory_space=pltpu.HBM)
    bf16 = jnp.bfloat16
    dma = pltpu.SemaphoreType.DMA
    result = pl.pallas_call(
        functools.partial(attend_kernel, (nx, nz, ny, caps, latents)),
        out_shape=jax.ShapeDtypeStruct((slot_count, latents, local_width), bf16),
        in_specs=[vmem, stay, vmem, stay, stay, stay, anywhere],
        out_specs=anywhere,
        scratch_shapes=[
            pltpu.VMEM((levels, patches, width), bf16),
            pltpu.VMEM((width, 2 * local_width), bf16),
            pltpu.VMEM((2, slot_count // nx, width), bf16),
            pltpu.VMEM((slot_count, patches), bf16),
            pltpu.VMEM((2, levels, slot_count // nx, local_width), bf16),
            pltpu.VMEM((2, levels, slot_count // nx, local_width), bf16),
            pltpu.VMEM((nx, chunk // latents, latents, local_width), bf16),
            pltpu.VMEM((nx, chunk, local_width), bf16),
            pltpu.VMEM((nx, ny - 1, share, local_width), bf16),
            pltpu.VMEM((ny, local_width, width), bf16),
            pltpu.VMEM((nx, ny, share // latents, latents, local_width), bf16),
            dma((levels,)),
            dma((2,)),
            dma,
            dma((nx,)),
            dma,
            dma((nx,)),
            dma((ny,)),
            dma((ny,)),
            dma((ny,)),
            dma((ny,)),
            dma,
            dma,
            pltpu.SemaphoreType.REGULAR,
            pltpu.SemaphoreType.REGULAR,
        ],
        compiler_params=pltpu.CompilerParams(
            collective_id=0, has_side_effects=True, vmem_limit_bytes=60 * 1024 * 1024
        ),
    )(
        send_slots.reshape(-1, caps).T,
        level_tokens.transpose(1, 0, 2),
        ln_gain.reshape(1, width),
        key_weight,
        value_weight,
        out_weight,
        ocean_queries,
    )
    return pl.pallas_call(
        hand_over_kernel,
        out_shape=jax.ShapeDtypeStruct(result.shape, bf16),
        in_specs=[anywhere],
        out_specs=anywhere,
        scratch_shapes=[pltpu.VMEM(result.shape, bf16), dma((PIECES,)), dma((PIECES,))],
        compiler_params=pltpu.CompilerParams(vmem_limit_bytes=60 * 1024 * 1024),
    )(result)


def solution(mesh):
    ny = mesh.shape["head"]
    nz = 2 * ny
    nx = mesh.shape["lat"] // (nz * CORES)
    return jax.shard_map(
        functools.partial(shards, (nx, nz, ny)),
        mesh=mesh,
        in_specs=(
            P("lat", None, None),
            P(),
            P(None, "head"),
            P(None, "head"),
            P("head", None),
            P("lat", None, "head"),
            P("lat", None, None),
        ),
        out_specs=P("lat", None, "head"),
        check_vma=False,
    )
```
